32 devices in a mesh: lon: 8 (over y, x, core), lat: 4 (over z).
Axes of the slice: x: 2, y: 2, z: 4, core: 2. Of those that a mesh axis runs over, the one named last changes fastest.
Arguments:
- ocean_state: float32 [3, 8, 64, 1024], P(None, None, 'lat', 'lon'), may hold values from -6 to 6
- diffusivity: float32 [8, 64, 1024], P(None, 'lat', 'lon'), may hold values from 0.02 to 0.22
- depth_levels: int32 [64, 1024], P('lat', 'lon'), may hold values from 0 to 8, as said below
- fold_pair: int32 [1024], replicated, may hold values from 0 to 1023, as said below
- first_weight: bfloat16 [9, 64, 24], replicated, may hold values from -0.4375 to 0.4375
- mix_weight: bfloat16 [64, 64], replicated, may hold values from -0.75 to 0.75
- last_weight: bfloat16 [9, 16, 64], replicated, may hold values from -0.25 to 0.25
- cotangent: bfloat16 [16, 64, 1024], P(None, 'lat', 'lon'), may hold values from -6 to 6
- active_index: int32 [8192], replicated, may hold values from 0 to 27135, as said below
Outputs:
- new_state: float32 [3, 8, 64, 1024], P(None, None, 'lat', 'lon')
- closure: bfloat16 [16, 64, 1024], P(None, 'lat', 'lon')
- grad_active: float32 [8192], replicated
The draws below stay inside these ranges and needn't reach their ends.
Inputs may be any that keep to these rules, and one draw needn't show every extreme that they name: `depth_levels`: 0 marks land; otherwise the number of wet levels of the column. fold_pair[i] = (s - i) mod 1024 for one s, the same for every i. `active_index`: distinct entries; 0 and 27135 are always among them.
All inputs are finite; a program needn't handle non-finite values.
Results may differ from the reference program's by a relative error of at most 0.0065.
Values may be sent and summed in bfloat16 or wider, within the bound.
A program may use at most 64 MiB of HBM per device.

```python
import math
import jax
import jax.numpy as jnp
from jax import lax

LEVELS = 8
CHANNELS = 64
LAT_DEV = 16
ACTIVE = 8192
NY = 64
NX = 1024
PARAMS = 27136
N_LAT = 4


def draw_ocean_state(key, part):
    key = jax.random.fold_in(key, 41)
    noise_key = jax.random.fold_in(key, 0)
    noise = jax.random.normal(noise_key, (3, LEVELS, NY, NX), jnp.float32)
    values = noise
    return jnp.clip(values, -6.0, 6.0).astype(jnp.float32)


def draw_diffusivity(key, part):
    key = jax.random.fold_in(key, 43)
    exponent = jax.random.uniform(key, (LEVELS, NY, NX), jnp.float32, math.log(0.02), math.log(0.22))
    values = jnp.exp(exponent)
    return jnp.clip(values, 0.02, 0.22).astype(jnp.float32)


def draw_depth_levels(key, part):
    key = jax.random.fold_in(key, 11)
    land_key, depth_key = jax.random.split(key)
    coast = jax.random.randint(land_key, (NY, NX), 0, 10)
    depth = jax.random.randint(depth_key, (NY, NX), 1, LEVELS + 1)
    return jnp.where(coast < 3, 0, depth).astype(jnp.int32)


def draw_fold_pair(key, part):
    key = jax.random.fold_in(key, 23)
    offset = jax.random.randint(key, (), 0, NX)
    return ((offset - jnp.arange(NX, dtype=jnp.int32)) % NX).astype(jnp.int32)


def draw_active_index(key, part):
    key = jax.random.fold_in(key, 37)
    first_key, order_key = jax.random.split(key)
    inner = jax.random.permutation(first_key, PARAMS - 2)[:ACTIVE - 2].astype(jnp.int32) + 1
    chosen = jnp.concatenate([inner, jnp.array([0, PARAMS - 1], jnp.int32)])
    return jax.random.permutation(order_key, chosen).astype(jnp.int32)


def shard_levels(own_key, shape, pieces, smallest, largest):
    level, own = 1.0, jax.random.fold_in(own_key, 6)
    for axis_at, shards_of in pieces:
        draws = jnp.exp(jax.random.uniform(jax.random.fold_in(own, axis_at), (shards_of,), jnp.float32, smallest / len(pieces), largest / len(pieces)))
        level = level * jnp.repeat(draws, shape[axis_at] // shards_of).reshape([-1 if axis == axis_at else 1 for axis in range(len(shape))])
    return level


def bell_draw(stream_key, extent, scale, reach, cuts=(), held_as=jnp.bfloat16):
    factor_of = shard_levels(stream_key, extent, cuts, -0.22, 0.18) if cuts else 1.0
    result = jax.random.normal(stream_key, extent, jnp.float32) * scale * factor_of
    return jnp.minimum(jnp.maximum(result, -reach), reach).astype(held_as)


def setup_inputs(seed: int = 0) -> dict:
    streams_of = jax.random.split(jax.random.key(seed), 10)
    ocean_state = draw_ocean_state(jax.random.fold_in(streams_of[9], 71), 0)
    diffusivity = draw_diffusivity(jax.random.fold_in(streams_of[9], 71), 0)
    depth_levels = draw_depth_levels(jax.random.fold_in(streams_of[9], 71), 0)
    fold_pair = draw_fold_pair(jax.random.fold_in(streams_of[9], 71), 0)
    first_weight = bell_draw(streams_of[4], (9, CHANNELS, 3 * LEVELS), (27 * LEVELS) ** -0.5, 0.4375)
    mix_weight = bell_draw(streams_of[5], (CHANNELS, CHANNELS), CHANNELS ** -0.5, 0.75)
    last_weight = bell_draw(streams_of[6], (9, 2 * LEVELS, CHANNELS), (9 * CHANNELS) ** -0.5, 0.25)
    cotangent = bell_draw(streams_of[7], (2 * LEVELS, NY, NX), 1.0, 6.0, ((1, 4), (2, 8)))
    active_index = draw_active_index(jax.random.fold_in(streams_of[9], 71), 0)
    return {"ocean_state": ocean_state, "diffusivity": diffusivity, "depth_levels": depth_levels, "fold_pair": fold_pair, "first_weight": first_weight, "mix_weight": mix_weight, "last_weight": last_weight, "cotangent": cotangent, "active_index": active_index}


coriolis_peak = 0.25
pressure_scale = 0.05
advect_scale = 0.25
highest = lax.Precision.HIGHEST

def coriolis(row_ids, row_total):
    mirrored = jnp.where(row_ids >= row_total, 2 * row_total - 1 - row_ids, row_ids)
    return coriolis_peak * jnp.sin(math.pi * (mirrored.astype(jnp.float32) + 0.5) / row_total - 0.5 * math.pi)

def offset_view(field, shift_row, shift_col):
    height = field.shape[1] - 2
    width = field.shape[2] - 2
    return field[:, 1 + shift_row:1 + shift_row + height, 1 + shift_col:1 + shift_col + width]

def stencil(padded, coriolis_rows):
    u_all = padded[0]
    v_all = padded[1]
    t_all = padded[2]
    k_all = padded[3]
    k_center = offset_view(k_all, 0, 0)
    k_east = jnp.sqrt(k_center * offset_view(k_all, 0, 1))
    k_west = jnp.sqrt(k_center * offset_view(k_all, 0, -1))
    k_north = jnp.sqrt(k_center * offset_view(k_all, 1, 0))
    k_south = jnp.sqrt(k_center * offset_view(k_all, -1, 0))

    def diffuse(field):
        middle = offset_view(field, 0, 0)
        return k_east * (offset_view(field, 0, 1) - middle) + k_west * (offset_view(field, 0, -1) - middle) + k_north * (offset_view(field, 1, 0) - middle) + k_south * (offset_view(field, -1, 0) - middle)
    pressure = pressure_scale * jnp.cumsum(t_all, axis=0)
    wet_here = (k_center > 0).astype(jnp.float32)
    f_rows = coriolis_rows[None, :, None]
    u_mid = offset_view(u_all, 0, 0)
    v_mid = offset_view(v_all, 0, 0)
    t_mid = offset_view(t_all, 0, 0)
    u_change = f_rows * v_mid - 0.5 * (offset_view(pressure, 0, 1) - offset_view(pressure, 0, -1))
    v_change = -f_rows * u_mid - 0.5 * (offset_view(pressure, 1, 0) - offset_view(pressure, -1, 0))
    t_change = -advect_scale * 0.5 * (u_mid * (offset_view(t_all, 0, 1) - offset_view(t_all, 0, -1)) + v_mid * (offset_view(t_all, 1, 0) - offset_view(t_all, -1, 0)))
    return jnp.stack([wet_here * (u_mid + u_change + diffuse(u_all)), wet_here * (v_mid + v_change + diffuse(v_all)), wet_here * (t_mid + t_change + diffuse(t_all))])

def pad_fold(field, fold_signs, fold_pair):
    col_total = field.shape[2]
    col_ids = ((jnp.arange(col_total + 2, dtype=jnp.int32) - 1) % col_total).astype(jnp.int32)
    wrapped = jnp.take(field, col_ids, axis=2)
    partner = jnp.take(fold_pair, col_ids).astype(jnp.int32)
    north_rows = fold_signs[:, None] * jnp.take(field[:, -1, :], partner, axis=1)
    south_rows = jnp.zeros_like(north_rows)
    return jnp.concatenate([south_rows[:, None], wrapped, north_rows[:, None]], axis=1)

def pad_open(field):
    col_total = field.shape[2]
    col_ids = ((jnp.arange(col_total + 2, dtype=jnp.int32) - 1) % col_total).astype(jnp.int32)
    wrapped = jnp.take(field, col_ids, axis=2)
    empty_row = jnp.zeros((field.shape[0], 1, col_total + 2), field.dtype)
    return jnp.concatenate([empty_row, wrapped, empty_row], axis=1)

def convolve(padded, weight):
    height = padded.shape[1] - 2
    width = padded.shape[2] - 2
    summed = None
    for tap_index in range(9):
        tap_row = tap_index // 3
        tap_col = tap_index % 3
        term = jnp.einsum('oc,cyx->oyx', weight[tap_index].astype(jnp.float32), padded[:, tap_row:tap_row + height, tap_col:tap_col + width].astype(jnp.float32), precision=highest)
        summed = term if tap_index == 0 else summed + term
    return summed

def convolve_back(padded, weight):
    height = padded.shape[1] - 2
    width = padded.shape[2] - 2
    summed = None
    for tap_index in range(9):
        tap_row = tap_index // 3
        tap_col = tap_index % 3
        term = jnp.einsum('oc,oyx->cyx', weight[tap_index].astype(jnp.float32), padded[:, 2 - tap_row:2 - tap_row + height, 2 - tap_col:2 - tap_col + width].astype(jnp.float32), precision=highest)
        summed = term if tap_index == 0 else summed + term
    return summed

def tap_grads(grad, padded):
    height = grad.shape[1]
    width = grad.shape[2]
    terms = []
    for tap_index in range(9):
        tap_row = tap_index // 3
        tap_col = tap_index % 3
        terms.append(jnp.einsum('oyx,cyx->oc', grad.astype(jnp.float32), padded[:, tap_row:tap_row + height, tap_col:tap_col + width].astype(jnp.float32), precision=highest))
    return jnp.stack(terms)

def silu_slope(pre):
    sigma = jax.nn.sigmoid(pre)
    return sigma * (1.0 + pre * (1.0 - sigma))

def reference(ocean_state, diffusivity, depth_levels, fold_pair, first_weight, mix_weight, last_weight, cotangent, active_index):
    level_ids = jnp.arange(LEVELS, dtype=jnp.int32)
    wet_mask = (level_ids[:, None, None] < depth_levels[None]).astype(jnp.float32)
    wet_kappa = diffusivity * wet_mask
    fields = ocean_state * wet_mask[None]
    fold_signs = jnp.concatenate([-jnp.ones((2 * LEVELS,), jnp.float32), jnp.ones((2 * LEVELS,), jnp.float32)])
    row_ids = jnp.arange(NY, dtype=jnp.int32)
    for step_index in range(2):
        stacked = jnp.concatenate([fields, wet_kappa[None]], axis=0).reshape(4 * LEVELS, NY, NX)
        padded = pad_fold(stacked, fold_signs, fold_pair).reshape(4, LEVELS, NY + 2, NX + 2)
        fields = stencil(padded, coriolis(row_ids, NY))
    new_state = fields
    inputs = new_state.reshape(3 * LEVELS, NY, NX).astype(jnp.bfloat16)
    level_mask = jnp.concatenate([wet_mask, wet_mask], axis=0)
    grad_scale = 1.0 / math.sqrt(NX * NY)
    out_grad = (grad_scale * level_mask * cotangent.astype(jnp.float32)).astype(jnp.bfloat16)
    x_pad = pad_open(inputs)
    g_pad = pad_open(out_grad)
    band_ids = jnp.arange(N_LAT, dtype=jnp.int32)

    def forward_band(band):
        window = lax.dynamic_slice_in_dim(x_pad, band * LAT_DEV, LAT_DEV + 2, 1)
        pre_first = convolve(window, first_weight)
        hidden_first = jax.nn.silu(pre_first).astype(jnp.bfloat16)
        pre_mix = jnp.einsum('oc,cyx->oyx', mix_weight.astype(jnp.float32), hidden_first.astype(jnp.float32), precision=highest)
        hidden_mix = jax.nn.silu(pre_mix).astype(jnp.bfloat16)
        return (window, pre_first, hidden_first, pre_mix, hidden_mix)
    hidden_bands = lax.map(lambda band: forward_band(band)[4], band_ids)
    hidden_all = jnp.transpose(hidden_bands, (1, 0, 2, 3)).reshape(CHANNELS, NY, NX)
    h_pad = pad_open(hidden_all)

    def backward_band(carry, band):
        window, pre_first, hidden_first, pre_mix, hidden_mix = forward_band(band)
        h_window = lax.dynamic_slice_in_dim(h_pad, band * LAT_DEV, LAT_DEV + 2, 1)
        g_window = lax.dynamic_slice_in_dim(g_pad, band * LAT_DEV, LAT_DEV + 2, 1)
        mask_band = lax.dynamic_slice_in_dim(level_mask, band * LAT_DEV, LAT_DEV, 1)
        grad_band = lax.dynamic_slice_in_dim(out_grad, band * LAT_DEV, LAT_DEV, 1)
        closure_band = (mask_band * convolve(h_window, last_weight)).astype(jnp.bfloat16)
        grad_last = tap_grads(grad_band, h_window)
        back_mix = convolve_back(g_window, last_weight)
        delta_mix = (back_mix * silu_slope(pre_mix)).astype(jnp.bfloat16)
        grad_mix = jnp.einsum('oyx,cyx->oc', delta_mix.astype(jnp.float32), hidden_first.astype(jnp.float32), precision=highest)
        back_first = jnp.einsum('oc,oyx->cyx', mix_weight.astype(jnp.float32), delta_mix.astype(jnp.float32), precision=highest)
        delta_first = (back_first * silu_slope(pre_first)).astype(jnp.bfloat16)
        grad_first = tap_grads(delta_first, window)
        return ((carry[0] + grad_first, carry[1] + grad_mix, carry[2] + grad_last), closure_band)
    start = (jnp.zeros((9, CHANNELS, 3 * LEVELS), jnp.float32), jnp.zeros((CHANNELS, CHANNELS), jnp.float32), jnp.zeros((9, 2 * LEVELS, CHANNELS), jnp.float32))
    totals, closure_bands = lax.scan(backward_band, start, band_ids)
    closure = jnp.transpose(closure_bands, (1, 0, 2, 3)).reshape(2 * LEVELS, NY, NX)
    flat = jnp.concatenate([totals[0].reshape(-1), totals[1].reshape(-1), totals[2].reshape(-1)])
    grad_active = jnp.take(flat, active_index.astype(jnp.int32))
    return (new_state, closure, grad_active)
```

```python
import functools
import math

import jax
import jax.numpy as jnp
from jax import lax
from jax.experimental import pallas as pl
from jax.experimental.pallas import tpu as pltpu
from jax.sharding import PartitionSpec as P

MESH = pl.DeviceIdType.MESH
F32 = jnp.float32
BF16 = jnp.bfloat16
WIDE = 4
VMEM = pl.BlockSpec(memory_space=pltpu.VMEM)
SMEM = pl.BlockSpec(memory_space=pltpu.SMEM)


def masked_row(ocean, kappa, depth, cot, row, scale):
    levels = lax.broadcasted_iota(jnp.int32, (8, 128), 0)
    wet = (levels < depth[pl.ds(row, 1), :]).astype(F32)
    u = ocean[0, :, row, :] * wet
    v = ocean[1, :, row, :] * wet
    t = ocean[2, :, row, :] * wet
    k = kappa[:, row, :] * wet
    wet2 = jnp.concatenate([wet, wet], axis=0)
    g = scale * wet2 * cot[row].astype(F32)
    return u, v, t, k, g, wet2


def exchange_kernel(
    n_lon, n_lat, scale, ocean, kappa, depth, cot, north, south, sides, tops,
    rows, packed, top_own, row_send, row_recv, side_send, side_recv, top_send, top_recv,
):
    lon = lax.axis_index("lon")
    lat = lax.axis_index("lat")
    count = rows.shape[0]
    east = lax.rem(lon + 1, n_lon)
    west = lax.rem(lon + n_lon - 1, n_lon)
    has_north = lat < n_lat - 1
    has_south = lat > 0
    at_top = lat == n_lat - 1

    barrier = pltpu.get_barrier_semaphore()

    def greet(to_lat, to_lon):
        pl.semaphore_signal(barrier, inc=1, device_id=(to_lon, to_lat), device_id_type=MESH)

    for step in range(1, n_lon):
        greet(lat, lax.rem(lon + step, n_lon))

    @pl.when(has_north)
    def _():
        for to in (lon, east, west):
            greet(lat + 1, to)

    @pl.when(has_south)
    def _():
        for to in (lon, east, west):
            greet(lat - 1, to)

    lanes = lax.broadcasted_iota(jnp.int32, (48, 128), 1)
    acc = jnp.zeros((48, 128), F32)
    for row in range(count):
        u, v, t, k, g, _ = masked_row(ocean, kappa, depth, cot, row, scale)
        line = jnp.concatenate([u, v, t, k, g], axis=0)
        rows[row] = line.astype(BF16)
        acc = jnp.where(lanes // 8 == row, pltpu.roll(line, (4 + 8 * row) % 128, axis=1), acc)
    packed[...] = acc.astype(BF16)

    sides_open = has_north.astype(jnp.int32) + has_south.astype(jnp.int32)
    pl.semaphore_wait(barrier, n_lon - 1 + 3 * sides_open)

    def send_rows(start, dst, slot, to_lat):
        return pltpu.make_async_remote_copy(
            src_ref=rows.at[pl.ds(start, WIDE)], dst_ref=dst, send_sem=row_send.at[slot],
            recv_sem=row_recv.at[slot], device_id=(lon, to_lat), device_id_type=MESH,
        )

    def send_side(slot, to_lat, to_lon):
        return pltpu.make_async_remote_copy(
            src_ref=packed, dst_ref=sides.at[slot], send_sem=side_send.at[slot],
            recv_sem=side_recv.at[slot], device_id=(to_lon, to_lat), device_id_type=MESH,
        )

    def send_top(step):
        return pltpu.make_async_remote_copy(
            src_ref=rows.at[pl.ds(count - 2, 2)], dst_ref=tops.at[lon], send_sem=top_send.at[step],
            recv_sem=top_recv.at[lon], device_id=(lax.rem(lon + step, n_lon), lat), device_id_type=MESH,
        )

    def top_from(step):
        peer = lax.rem(lon + step, n_lon)
        return pltpu.make_async_remote_copy(
            src_ref=rows.at[pl.ds(count - 2, 2)], dst_ref=tops.at[peer], send_sem=top_send.at[step],
            recv_sem=top_recv.at[peer], device_id=(peer, lat), device_id_type=MESH,
        )

    to_north = send_rows(count - WIDE, south, 0, lat + 1)
    to_south = send_rows(0, north, 1, lat - 1)
    same = [send_side(0, lat, east), send_side(1, lat, west)]
    up = [send_side(2, lat + 1, east), send_side(3, lat + 1, west)]
    down = [send_side(4, lat - 1, east), send_side(5, lat - 1, west)]

    @pl.when(has_north)
    def _():
        to_north.start()

    @pl.when(has_south)
    def _():
        to_south.start()

    @pl.when(at_top)
    def _():
        for step in range(1, n_lon):
            send_top(step).start()

    for copy in same:
        copy.start()

    @pl.when(has_north)
    def _():
        for copy in up:
            copy.start()

    @pl.when(has_south)
    def _():
        for copy in down:
            copy.start()

    for copy in same:
        copy.wait()

    @pl.when(has_north)
    def _():
        to_north.wait_send()
        to_south.wait_recv()
        for copy in up:
            copy.wait_send()
        for copy in down:
            copy.wait_recv()

    @pl.when(has_south)
    def _():
        to_south.wait_send()
        to_north.wait_recv()
        for copy in down:
            copy.wait_send()
        for copy in up:
            copy.wait_recv()

    @pl.when(at_top)
    def _():
        tops[lon] = rows[count - 2 : count]
        for step in range(1, n_lon):
            send_top(step).wait_send()
            top_from(step).wait_recv()


def dot(a, b):
    return jnp.dot(a, b, preferred_element_type=F32)


def dot_cells(a, b):
    return lax.dot_general(a, b, (((1,), (1,)), ((), ())), preferred_element_type=F32)


def slope(pre, sigma):
    return sigma * (1.0 + pre * (1.0 - sigma))


def sigmoid(pre):
    return 1.0 / (1.0 + jnp.exp(-pre))


def east_of(own, rim, lane):
    a = pltpu.roll(own, 127, axis=own.ndim - 1)
    b = pltpu.roll(rim, 127, axis=own.ndim - 1)
    return jnp.where(lane == 127, b, a), jnp.where(lane == 127, a, b)


def west_of(own, rim, lane):
    a = pltpu.roll(own, 1, axis=own.ndim - 1)
    b = pltpu.roll(rim, 1, axis=own.ndim - 1)
    return jnp.where(lane == 0, b, a), jnp.where(lane == 0, a, b)


def compute_kernel(
    n_lon, n_lat, scale, fold, ocean, kappa, depth, cot, north, south, sides, tops,
    w_first, w_mix, w_mix_t, w_last, w_back, krow, klane, coriolis,
    state, closure, picked,
    f_a, f_b, h_a, h_b, ks_a, ks_b, g_own, wet2s, patches, slope1, slope2, hid1, hid2, hshift, gpatch, dmix, dfirst, table,
):
    lon = lax.axis_index("lon")
    lat = lax.axis_index("lat")
    count = ocean.shape[2]
    total = count + 2 * WIDE
    at_top = lat == n_lat - 1
    at_bottom = lat == 0
    lane = lax.broadcasted_iota(jnp.int32, (8, 128), 1)
    level = lax.broadcasted_iota(jnp.int32, (8, 128), 0)
    lane48 = lax.broadcasted_iota(jnp.int32, (48, 128), 1)
    zero48 = jnp.zeros((48, 128), F32)

    def merge(low):
        odd = lane48 % 8 >= 4
        return jnp.where(odd, sides[low + 1].astype(F32), sides[low].astype(F32))

    def put(row, own, rim):
        for f in range(4):
            if own is not None:
                f_a[row, f] = own[8 * f : 8 * f + 8]
            f_b[row, f] = rim[8 * f : 8 * f + 8]
        if WIDE - 1 <= row <= WIDE + count:
            if own is not None:
                g_own[row - WIDE + 1, 0] = own[32:48]
            g_own[row - WIDE + 1, 1] = rim[32:48]

    def unpack(side, row):
        return pltpu.roll(side, (128 - 4 - 8 * row) % 128, axis=1)

    mid = merge(0)
    below = jnp.where(at_bottom, zero48, merge(2))
    above = jnp.where(at_top, zero48, merge(4))
    for row in range(count):
        u, v, t, k, g, wet2 = masked_row(ocean, kappa, depth, cot, row, scale)
        own = jnp.concatenate([u, v, t, k, g.astype(BF16).astype(F32)], axis=0)
        put(row + WIDE, own, unpack(mid, row))
        wet2s[row] = wet2
    for row in range(WIDE):
        put(row, jnp.where(at_bottom, zero48, south[row].astype(F32)), unpack(below, count - WIDE + row))
        put(WIDE + count + row, jnp.where(at_top, zero48, north[row].astype(F32)), unpack(above, row))

    @pl.when(at_top)
    def _():
        nx = n_lon * 128
        s = fold[0]
        at = lax.broadcasted_iota(jnp.int32, (128, 256), 0)
        pos = lax.broadcasted_iota(jnp.int32, (1, 256), 1)
        col = lon * 128 + jnp.where(pos >= 192, pos - 256, pos)
        col = jnp.where(col < 0, col + nx, col)
        col = jnp.where(col >= nx, col - nx, col)
        partner = s - col
        partner = jnp.where(partner < 0, partner + nx, partner)
        res = jnp.zeros((64, 256), F32)
        for j in range(n_lon):
            pick = jnp.where(at + 128 * j == partner, 1.0, 0.0).astype(BF16)
            both = jnp.concatenate([tops[j, 1, 0:32], tops[j, 0, 0:32]], axis=0)
            res = res + dot(both, pick)
        for q in range(2):
            for f in range(4):
                sign = -1.0 if f < 2 else 1.0
                part = sign * res[32 * q + 8 * f : 32 * q + 8 * f + 8]
                f_a[WIDE + count + q, f] = part[:, :128]
                f_b[WIDE + count + q, f] = part[:, 128:]

    def roots(r, _):
        k_a, k_b = f_a[r, 3], f_b[r, 3]
        e_a, e_b = east_of(k_a, k_b, lane)
        ks_a[r, 0] = jnp.sqrt(k_a * e_a)
        ks_b[r, 0] = jnp.sqrt(k_b * e_b)
        ks_a[r, 1] = jnp.sqrt(k_a * f_a[r + 1, 3])
        ks_b[r, 1] = jnp.sqrt(k_b * f_b[r + 1, 3])
        return 0

    lax.fori_loop(0, total - 1, roots, 0, unroll=2)

    def summed(x):
        for d in (1, 2, 4):
            x = x + jnp.where(level >= d, pltpu.roll(x, d, axis=0), 0.0)
        return x

    def step(src_a, src_b, dst_a, dst_b):
        def body(r, _):
            fr = coriolis[r]
            ke_a, ke_b = ks_a[r, 0], ks_b[r, 0]
            kw_a, kw_b = west_of(ke_a, ke_b, lane)
            coef = ((ke_a, kw_a, ks_a[r, 1], ks_a[r - 1, 1]), (ke_b, kw_b, ks_b[r, 1], ks_b[r - 1, 1]))
            mids, es, ws = [], [], []
            for f in range(3):
                a, b = src_a[r, f], src_b[r, f]
                mids.append((a, b))
                es.append(east_of(a, b, lane))
                ws.append(west_of(a, b, lane))
            for i, (src, dst, k_own) in enumerate(((src_a, dst_a, f_a[r, 3]), (src_b, dst_b, f_b[r, 3]))):
                wet = jnp.where(k_own > 0, 1.0, 0.0)
                ke, kw, kn, ks = coef[i]
                u, v, t = mids[0][i], mids[1][i], mids[2][i]
                ns = [src[r + 1, f] for f in range(3)]
                ss = [src[r - 1, f] for f in range(3)]
                outs = []
                for f in range(3):
                    m = mids[f][i]
                    outs.append(
                        m + ke * (es[f][i] - m) + kw * (ws[f][i] - m) + kn * (ns[f] - m) + ks * (ss[f] - m)
                    )
                dx = es[2][i] - ws[2][i]
                dy = ns[2] - ss[2]
                dst[r, 0] = wet * (outs[0] + fr * v - 0.025 * summed(dx))
                dst[r, 1] = wet * (outs[1] - fr * u - 0.025 * summed(dy))
                dst[r, 2] = wet * (outs[2] - 0.125 * (u * dx + v * dy))
            return 0

        return body

    lax.fori_loop(1, total - 1, step(f_a, f_b, h_a, h_b), 0, unroll=2)
    lax.fori_loop(2, total - 2, step(h_a, h_b, f_a, f_b), 0, unroll=2)
    for row in range(count):
        for f in range(3):
            state[f, :, row, :] = f_a[row + WIDE, f]

    lane24 = lax.broadcasted_iota(jnp.int32, (24, 128), 1)
    lane72 = lax.broadcasted_iota(jnp.int32, (72, 128), 1)
    pad8 = jnp.zeros((8, 128), F32)
    lines = []
    side = jnp.zeros((72, 128), F32)
    for q in range(count + 4):
        a = jnp.concatenate([f_a[q + 2, f] for f in range(3)], axis=0)
        b = jnp.concatenate([f_b[q + 2, f] for f in range(3)], axis=0)
        if q < 2:
            a, b = jnp.where(at_bottom, 0.0, a), jnp.where(at_bottom, 0.0, b)
        if q >= count + 2:
            a, b = jnp.where(at_top, 0.0, a), jnp.where(at_top, 0.0, b)
        e_a, e_b = east_of(a, b, lane24)
        w_a, w_b = west_of(a, b, lane24)
        lines.append(jnp.concatenate([w_a, a, e_a], axis=0))
        rim = jnp.concatenate([w_b, b, e_b], axis=0)
        side = jnp.where(lane72 // 2 == q, pltpu.roll(rim, (1 + 2 * q) % 128, axis=1), side)
        if q >= 2:
            r = q - 2
            patches[:, 128 * r : 128 * r + 128] = jnp.concatenate(lines[-3:] + [pad8], axis=0).astype(BF16)
    span = (count + 2) * 128
    patches[:, span : span + 128] = jnp.concatenate(
        [side, pltpu.roll(side, 126, axis=1), pltpu.roll(side, 124, axis=1), pad8], axis=0
    ).astype(BF16)
    patches[:, span + 128 :] = jnp.zeros((224, patches.shape[1] - span - 128), BF16)

    for start in range(0, patches.shape[1], 256):
        pre1 = dot(w_first[...], patches[:, start : start + 256])
        s1 = sigmoid(pre1)
        h1 = (pre1 * s1).astype(BF16)
        pre2 = dot(w_mix[...], h1)
        s2 = sigmoid(pre2)
        hid1[:, start : start + 256] = h1
        hid2[:, start : start + 256] = (pre2 * s2).astype(BF16).astype(F32)
        slope1[:, start : start + 256] = slope(pre1, s1)
        slope2[:, start : start + 256] = slope(pre2, s2)

    lane64 = lax.broadcasted_iota(jnp.int32, (64, 128), 1)
    lane16 = lax.broadcasted_iota(jnp.int32, (16, 128), 1)
    edge = hid2[:, span : span + 128]
    for r in range(count + 2):
        own = hid2[:, 128 * r : 128 * r + 128]
        to_w = jnp.where(lane64 == 0, pltpu.roll(edge, (128 - 2 * r) % 128, axis=1), pltpu.roll(own, 1, axis=1))
        to_e = jnp.where(lane64 == 127, pltpu.roll(edge, 126 - 2 * r, axis=1), pltpu.roll(own, 127, axis=1))
        both = jnp.concatenate([to_w, own, to_e], axis=0)
        if r == 0:
            both = jnp.where(at_bottom, 0.0, both)
        if r == count + 1:
            both = jnp.where(at_top, 0.0, both)
        hshift[:, 128 * r : 128 * r + 128] = both.astype(BF16)
    glines = []
    for r in range(count + 2):
        a, b = g_own[r, 0], g_own[r, 1]
        e_a, _ = east_of(a, b, lane16)
        w_a, _ = west_of(a, b, lane16)
        glines.append(jnp.concatenate([e_a, a, w_a], axis=0))
        if r >= 2:
            j = r - 2
            gpatch[:, 128 * j : 128 * j + 128] = jnp.concatenate(glines[-3:][::-1], axis=0).astype(BF16)

    cells = count * 128
    for start in range(0, cells, 256):
        here = slice(start, start + 256)
        near = slice(start + 128, start + 384)
        out = dot(w_last[0], hshift[:, start : start + 256])
        out += dot(w_last[1], hshift[:, start + 128 : start + 384])
        out += dot(w_last[2], hshift[:, start + 256 : start + 512])
        for j in range(2):
            r = start // 128 + j
            closure[r] = (wet2s[r] * out[:, 128 * j : 128 * j + 128]).astype(BF16)
        back = dot(w_back[...], gpatch[:, here])
        dm = (back * slope2[:, near]).astype(BF16)
        dmix[:, here] = dm
        dfirst[:, here] = (dot(w_mix_t[...], dm) * slope1[:, near]).astype(BF16)

    g_first = dot_cells(dfirst[...], patches[:, 128 : 128 + cells])
    g_mix = dot_cells(dmix[...], hid1[:, 128 : 128 + cells])
    g_mid = gpatch[64:80, :]
    g_last = jnp.concatenate([dot_cells(g_mid, hshift[:, 128 * i : 128 * i + cells]) for i in range(3)], axis=1)
    table[0:64, :] = g_first[:, :128]
    table[64:128, 0:96] = g_first[:, 128:224]
    table[64:128, 96:128] = jnp.zeros((64, 32), F32)
    table[128:192, 64:128] = jnp.zeros((64, 64), F32)
    table[128:192, 0:64] = g_mix
    table[128:144, 64:128] = g_last[:, 512:576]
    for i in range(4):
        table[192 + 16 * i : 208 + 16 * i, :] = g_last[:, 128 * i : 128 * i + 128]
    q = table[...].T
    hi = q.astype(BF16)
    lo = (q - hi.astype(F32)).astype(BF16)
    split = jnp.concatenate([hi, lo], axis=0)
    at_row = lax.broadcasted_iota(jnp.int32, (256, 128), 0)
    at_lane = lax.broadcasted_iota(jnp.int32, (128, 128), 0)
    for j in range(0, krow.shape[0], 2):
        pick = jnp.concatenate(
            [jnp.where(at_row == krow[j + i : j + i + 1, :], 1.0, 0.0).astype(BF16) for i in range(2)], axis=1
        )
        got = dot(split, pick)
        got = got[:128] + got[128:]
        for i in range(2):
            mine = jnp.where(at_lane == klane[j + i : j + i + 1, :], got[:, 128 * i : 128 * i + 128], 0.0)
            picked[j + i : j + i + 1, :] = jnp.sum(mine, axis=0, keepdims=True)


def reduce_kernel(n_lon, n_lat, part, out, got_lon, got_lat, chunk, s1, r1, s2, r2, s3, r3):
    lon = lax.axis_index("lon")
    lat = lax.axis_index("lat")
    barrier = pltpu.get_barrier_semaphore()
    lons = [lax.rem(lon + step, n_lon) for step in range(1, n_lon)]
    lats = [lax.rem(lat + step, n_lat) for step in range(1, n_lat)]
    for to in lons:
        pl.semaphore_signal(barrier, inc=1, device_id=(to, lat), device_id_type=MESH)
    for to in lats:
        pl.semaphore_signal(barrier, inc=1, device_id=(lon, to), device_id_type=MESH)
    pl.semaphore_wait(barrier, n_lon + n_lat - 2)

    def copy(src, dst, ssem, rsem, to):
        return pltpu.make_async_remote_copy(
            src_ref=src, dst_ref=dst, send_sem=ssem, recv_sem=rsem, device_id=to, device_id_type=MESH
        )

    first = [copy(part.at[to], got_lon.at[lon], s1.at[to], r1.at[lon], (to, lat)) for to in lons]
    for c in first:
        c.start()
    got_lon[lon] = part[lon]
    for c, to in zip(first, lons):
        c.wait_send()
        copy(part.at[to], got_lon.at[to], s1.at[to], r1.at[to], (to, lat)).wait_recv()
    got_lat[lat] = jnp.sum(got_lon[...], axis=0)
    second = [copy(got_lat.at[lat], got_lat.at[lat], s2.at[to], r2.at[lat], (lon, to)) for to in lats]
    for c in second:
        c.start()
    for c, to in zip(second, lats):
        c.wait_send()
        copy(got_lat.at[to], got_lat.at[to], s2.at[to], r2.at[to], (lon, to)).wait_recv()
    chunk[...] = jnp.sum(got_lat[...], axis=0)
    third = [copy(chunk, out.at[lon], s3.at[to], r3.at[lon], (to, lat)) for to in lons]
    for c in third:
        c.start()
    out[lon] = chunk[...]
    for c, to in zip(third, lons):
        c.wait_send()
        copy(chunk, out.at[to], s3.at[to], r3.at[to], (to, lat)).wait_recv()


def entry_place(index):
    k, rest = index // 1536, index % 1536
    col = (k * 24) + rest % 24
    row_f, lane_f = rest // 24 + 64 * (col // 128), col % 128
    m = index - 13824
    row_m, lane_m = 128 + m // 64, m % 64
    m = index - 17920
    o, col = (m % 1024) // 64, (m // 1024) * 64 + m % 64
    spill = col >= 512
    row_l = jnp.where(spill, 128 + o, 192 + 16 * (col // 128) + o)
    lane_l = jnp.where(spill, 64 + col - 512, col % 128)
    row = jnp.where(index < 13824, row_f, jnp.where(index < 17920, row_m, row_l))
    lane = jnp.where(index < 13824, lane_f, jnp.where(index < 17920, lane_m, lane_l))
    return row, lane


def on_device(
    n_lon, n_lat, ocean_state, diffusivity, depth_levels, fold_pair, first_weight, mix_weight, last_weight,
    cotangent, active_index,
):
    count = ocean_state.shape[2]
    row_total = count * n_lat
    scale = 1.0 / math.sqrt(row_total * 128 * n_lon)
    cot = jnp.transpose(cotangent, (1, 0, 2))
    sds = jax.ShapeDtypeStruct
    dma = pltpu.SemaphoreType.DMA
    north, south, sides, tops = pl.pallas_call(
        functools.partial(exchange_kernel, n_lon, n_lat, scale),
        out_shape=[
            sds((WIDE, 48, 128), BF16), sds((WIDE, 48, 128), BF16), sds((6, 48, 128), BF16),
            sds((n_lon, 2, 48, 128), BF16),
        ],
        in_specs=[VMEM] * 4,
        out_specs=[VMEM] * 4,
        scratch_shapes=[
            pltpu.VMEM((count, 48, 128), BF16), pltpu.VMEM((48, 128), BF16), pltpu.VMEM((2, 48, 128), BF16),
            dma((2,)), dma((2,)), dma((6,)), dma((6,)), dma((n_lon,)), dma((n_lon,)),
        ],
        compiler_params=pltpu.CompilerParams(collective_id=0, has_side_effects=True),
        name="exchange",
    )(ocean_state, diffusivity, depth_levels, cot)

    row_ids = lax.axis_index("lat") * count - WIDE + jnp.arange(count + 2 * WIDE, dtype=jnp.int32)
    mirrored = jnp.where(row_ids >= row_total, 2 * row_total - 1 - row_ids, row_ids)
    rows_f = 0.25 * jnp.sin(math.pi * (mirrored.astype(F32) + 0.5) / row_total - 0.5 * math.pi)
    w_first = jnp.pad(jnp.transpose(first_weight, (1, 0, 2)).reshape(64, 216), ((0, 0), (0, 8)))
    w_last = jnp.transpose(last_weight.reshape(3, 3, 16, 64), (0, 2, 1, 3)).reshape(3, 16, 192)
    w_back = jnp.transpose(last_weight, (2, 0, 1)).reshape(64, 144)
    krow, klane = entry_place(active_index)
    picks = active_index.shape[0] // 128
    total = count + 2 * WIDE
    wide = (count + 4) * 128
    cells = count * 128
    state, closure, picked = pl.pallas_call(
        functools.partial(compute_kernel, n_lon, n_lat, scale),
        out_shape=[
            sds((3, 8, count, 128), F32), sds((count, 16, 128), BF16), sds((picks, 128), F32),
        ],
        in_specs=[SMEM] + [VMEM] * 15 + [SMEM],
        out_specs=[VMEM] * 3,
        scratch_shapes=[
            pltpu.VMEM((total, 4, 8, 128), F32), pltpu.VMEM((total, 4, 8, 128), F32),
            pltpu.VMEM((total, 3, 8, 128), F32), pltpu.VMEM((total, 3, 8, 128), F32),
            pltpu.VMEM((total, 2, 8, 128), F32), pltpu.VMEM((total, 2, 8, 128), F32),
            pltpu.VMEM((count + 2, 2, 16, 128), F32), pltpu.VMEM((count, 16, 128), F32),
            pltpu.VMEM((224, wide), BF16), pltpu.VMEM((64, wide), F32), pltpu.VMEM((64, wide), F32),
            pltpu.VMEM((64, wide), BF16), pltpu.VMEM((64, wide), F32), pltpu.VMEM((192, (count + 2) * 128), BF16),
            pltpu.VMEM((144, cells), BF16), pltpu.VMEM((64, cells), BF16), pltpu.VMEM((64, cells), BF16),
            pltpu.VMEM((256, 128), F32),
        ],
        compiler_params=pltpu.CompilerParams(vmem_limit_bytes=48 * 1024 * 1024),
        name="compute",
    )(
        fold_pair[:8], ocean_state, diffusivity, depth_levels, cot, north, south, sides, tops, w_first, mix_weight,
        mix_weight.T, w_last, w_back, krow.reshape(picks, 128), klane.reshape(picks, 128), rows_f,
    )

    depth = picks // n_lon
    reduced = pl.pallas_call(
        functools.partial(reduce_kernel, n_lon, n_lat),
        out_shape=sds((n_lon, depth, 128), F32),
        in_specs=[VMEM],
        out_specs=VMEM,
        scratch_shapes=[
            pltpu.VMEM((n_lon, depth, 128), F32), pltpu.VMEM((n_lat, depth, 128), F32), pltpu.VMEM((depth, 128), F32),
            dma((n_lon,)), dma((n_lon,)), dma((n_lat,)), dma((n_lat,)), dma((n_lon,)), dma((n_lon,)),
        ],
        compiler_params=pltpu.CompilerParams(collective_id=1, has_side_effects=True),
        name="reduce",
    )(picked.reshape(n_lon, depth, 128))
    return state, jnp.transpose(closure, (1, 0, 2)), reduced.reshape(-1)


def solution(mesh):
    in_specs = (
        P(None, None, "lat", "lon"), P(None, "lat", "lon"), P("lat", "lon"), P(), P(), P(), P(),
        P(None, "lat", "lon"), P(),
    )
    out_specs = (P(None, None, "lat", "lon"), P(None, "lat", "lon"), P())
    return jax.shard_map(
        functools.partial(on_device, mesh.shape["lon"], mesh.shape["lat"]),
        mesh=mesh, in_specs=in_specs, out_specs=out_specs, check_vma=False,
    )
```

```python
import functools
import math

import jax
import jax.numpy as jnp
from jax import lax
from jax.experimental import pallas as pl
from jax.experimental.pallas import tpu as pltpu
from jax.sharding import PartitionSpec as P

MESH = pl.DeviceIdType.MESH
F32 = jnp.float32
BF16 = jnp.bfloat16
WIDE = 4
VMEM = pl.BlockSpec(memory_space=pltpu.VMEM)
SMEM = pl.BlockSpec(memory_space=pltpu.SMEM)


def masked_row(ocean, kappa, depth, cot, row, scale):
    levels = lax.broadcasted_iota(jnp.int32, (8, 128), 0)
    wet = (levels < depth[pl.ds(row, 1), :]).astype(F32)
    u = ocean[0, :, row, :] * wet
    v = ocean[1, :, row, :] * wet
    t = ocean[2, :, row, :] * wet
    k = kappa[:, row, :] * wet
    wet2 = jnp.concatenate([wet, wet], axis=0)
    g = scale * wet2 * cot[:, row, :]
    return u, v, t, k, g, wet2


def dot(a, b):
    return jnp.dot(a, b, preferred_element_type=F32)


def dot_cells(a, b):
    return lax.dot_general(a, b, (((1,), (1,)), ((), ())), preferred_element_type=F32)


def slope(pre, sigma):
    return sigma * (1.0 + pre * (1.0 - sigma))


def sigmoid(pre):
    return 1.0 / (1.0 + jnp.exp(-pre))


def east_of(own, rim, lane):
    a = pltpu.roll(own, 127, axis=own.ndim - 1)
    b = pltpu.roll(rim, 127, axis=own.ndim - 1)
    return jnp.where(lane == 127, b, a), jnp.where(lane == 127, a, b)


def west_of(own, rim, lane):
    a = pltpu.roll(own, 1, axis=own.ndim - 1)
    b = pltpu.roll(rim, 1, axis=own.ndim - 1)
    return jnp.where(lane == 0, b, a), jnp.where(lane == 0, a, b)


def kernel(
    n_lon, n_lat, scale, fold, ocean, kappa, depth, cot_in, first_w, mix_w, last_w, krow, klane, coriolis,
    state, closure, out,
    cot, closing, north, south, sides, tops, rows, packed, partner_pick, picks, w_first, w_last, w_back, w_mix_t,
    f_a, f_b, h_a, h_b, ks_a, ks_b, g_own, wet2s, patches, slope1, slope2, hid1, hid2, hshift, gpatch, dmix, dfirst, table,
    picked, got_lon, got_lat, chunk,
    row_send, row_recv, side_send, side_recv, top_send, top_recv, out_sem1, in_sem1, out_sem2, in_sem2, out_sem3, in_sem3,
):
    lon = lax.axis_index("lon")
    lat = lax.axis_index("lat")
    count = rows.shape[0]
    east = lax.rem(lon + 1, n_lon)
    west = lax.rem(lon + n_lon - 1, n_lon)
    has_north = lat < n_lat - 1
    has_south = lat > 0
    at_top = lat == n_lat - 1

    barrier = pltpu.get_barrier_semaphore()

    def greet(to_lat, to_lon):
        pl.semaphore_signal(barrier, inc=1, device_id=(to_lon, to_lat), device_id_type=MESH)

    for step in range(1, n_lon):
        greet(lat, lax.rem(lon + step, n_lon))
    for step in range(1, n_lat):
        greet(lax.rem(lat + step, n_lat), lon)
    cot[...] = cot_in[...].astype(F32)

    @pl.when(has_north)
    def _():
        for to in (east, west):
            greet(lat + 1, to)

    @pl.when(has_south)
    def _():
        for to in (east, west):
            greet(lat - 1, to)

    lanes = lax.broadcasted_iota(jnp.int32, (48, 128), 1)
    acc = jnp.zeros((48, 128), F32)
    for row in range(count):
        u, v, t, k, g, wet2 = masked_row(ocean, kappa, depth, cot, row, scale)
        line = jnp.concatenate([u, v, t, k, g], axis=0)
        for f, field in enumerate((u, v, t, k)):
            f_a[row + WIDE, f] = field
        g_own[row + 1, 0] = g.astype(BF16).astype(F32)
        wet2s[row] = wet2
        rows[row] = line.astype(BF16)
        acc = jnp.where(lanes // 8 == row, pltpu.roll(line, (4 + 8 * row) % 128, axis=1), acc)
    packed[...] = acc.astype(BF16)

    sides_open = has_north.astype(jnp.int32) + has_south.astype(jnp.int32)
    pl.semaphore_wait(barrier, n_lon + n_lat - 2 + 2 * sides_open)

    def send_rows(start, dst, slot, to_lat):
        return pltpu.make_async_remote_copy(
            src_ref=rows.at[pl.ds(start, WIDE)], dst_ref=dst, send_sem=row_send.at[slot],
            recv_sem=row_recv.at[slot], device_id=(lon, to_lat), device_id_type=MESH,
        )

    def send_side(slot, to_lat, to_lon):
        return pltpu.make_async_remote_copy(
            src_ref=packed, dst_ref=sides.at[slot], send_sem=side_send.at[slot],
            recv_sem=side_recv.at[slot], device_id=(to_lon, to_lat), device_id_type=MESH,
        )

    def send_top(step):
        return pltpu.make_async_remote_copy(
            src_ref=rows.at[pl.ds(count - 2, 2)], dst_ref=tops.at[lon], send_sem=top_send.at[step],
            recv_sem=top_recv.at[lon], device_id=(lax.rem(lon + step, n_lon), lat), device_id_type=MESH,
        )

    def top_from(step):
        peer = lax.rem(lon + step, n_lon)
        return pltpu.make_async_remote_copy(
            src_ref=rows.at[pl.ds(count - 2, 2)], dst_ref=tops.at[peer], send_sem=top_send.at[step],
            recv_sem=top_recv.at[peer], device_id=(peer, lat), device_id_type=MESH,
        )

    to_north = send_rows(count - WIDE, south, 0, lat + 1)
    to_south = send_rows(0, north, 1, lat - 1)
    same = [send_side(0, lat, east), send_side(1, lat, west)]
    up = [send_side(2, lat + 1, east), send_side(3, lat + 1, west)]
    down = [send_side(4, lat - 1, east), send_side(5, lat - 1, west)]

    @pl.when(has_north)
    def _():
        to_north.start()

    @pl.when(has_south)
    def _():
        to_south.start()

    @pl.when(at_top)
    def _():
        for step in range(1, n_lon):
            send_top(step).start()

    for copy in same:
        copy.start()

    @pl.when(has_north)
    def _():
        for copy in up:
            copy.start()

    @pl.when(has_south)
    def _():
        for copy in down:
            copy.start()


    def placed(height, width, shift):
        at = lax.broadcasted_iota(jnp.int32, (height, width), 0)
        to = lax.broadcasted_iota(jnp.int32, (height, width), 1)
        return jnp.where(at + shift == to, 1.0, 0.0).astype(BF16)

    wide_w = dot(first_w[0], placed(24, 224, 0))
    for k in range(1, 9):
        wide_w += dot(first_w[k], placed(24, 224, 24 * k))
    w_first[...] = wide_w.astype(BF16)
    for k in range(3):
        w_last[k] = sum(dot(last_w[3 * k + i], placed(64, 192, 64 * i)) for i in range(3)).astype(BF16)
    back_w = jnp.concatenate([last_w[k].astype(F32) for k in range(9)], axis=0)
    w_back[...] = back_w.T.astype(BF16)
    w_mix_t[...] = mix_w[...].astype(F32).T.astype(BF16)
    at_row = lax.broadcasted_iota(jnp.int32, (256, 128), 0)
    at_lane = lax.broadcasted_iota(jnp.int32, (128, 128), 0)
    for j in range(krow.shape[0]):
        picks[:, 128 * j : 128 * j + 128] = jnp.where(at_row == krow[j : j + 1, :], 1.0, 0.0).astype(BF16)

    @pl.when(at_top)
    def _():
        nx = n_lon * 128
        s = fold[0]
        at = lax.broadcasted_iota(jnp.int32, (128, 256), 0)
        pos = lax.broadcasted_iota(jnp.int32, (1, 256), 1)
        col = lon * 128 + jnp.where(pos >= 192, pos - 256, pos)
        col = jnp.where(col < 0, col + nx, col)
        col = jnp.where(col >= nx, col - nx, col)
        partner = s - col
        partner = jnp.where(partner < 0, partner + nx, partner)
        for j in range(n_lon):
            partner_pick[j] = jnp.where(at + 128 * j == partner, 1.0, 0.0).astype(BF16)

    for copy in same:
        copy.wait()

    @pl.when(has_north)
    def _():
        to_north.wait_send()
        to_south.wait_recv()
        for copy in up:
            copy.wait_send()
        for copy in down:
            copy.wait_recv()

    @pl.when(has_south)
    def _():
        to_south.wait_send()
        to_north.wait_recv()
        for copy in down:
            copy.wait_send()
        for copy in up:
            copy.wait_recv()

    @pl.when(at_top)
    def _():
        tops[lon] = rows[count - 2 : count]
        for step in range(1, n_lon):
            send_top(step).wait_send()
            top_from(step).wait_recv()

    total = count + 2 * WIDE
    at_bottom = lat == 0
    lane = lax.broadcasted_iota(jnp.int32, (8, 128), 1)
    level = lax.broadcasted_iota(jnp.int32, (8, 128), 0)
    lane48 = lax.broadcasted_iota(jnp.int32, (48, 128), 1)
    zero48 = jnp.zeros((48, 128), F32)

    def merge(low):
        odd = lane48 % 8 >= 4
        return jnp.where(odd, sides[low + 1].astype(F32), sides[low].astype(F32))

    def put(row, own, rim):
        for f in range(4):
            if own is not None:
                f_a[row, f] = own[8 * f : 8 * f + 8]
            f_b[row, f] = rim[8 * f : 8 * f + 8]
        if WIDE - 1 <= row <= WIDE + count:
            if own is not None:
                g_own[row - WIDE + 1, 0] = own[32:48]
            g_own[row - WIDE + 1, 1] = rim[32:48]

    def unpack(side, row):
        return pltpu.roll(side, (128 - 4 - 8 * row) % 128, axis=1)

    mid = merge(0)
    below = jnp.where(at_bottom, zero48, merge(2))
    above = jnp.where(at_top, zero48, merge(4))
    for row in range(count):
        put(row + WIDE, None, unpack(mid, row))
    for row in range(WIDE):
        put(row, jnp.where(at_bottom, zero48, south[row].astype(F32)), unpack(below, count - WIDE + row))
        put(WIDE + count + row, jnp.where(at_top, zero48, north[row].astype(F32)), unpack(above, row))

    @pl.when(at_top)
    def _():
        res = jnp.zeros((64, 256), F32)
        for j in range(n_lon):
            both = jnp.concatenate([tops[j, 1, 0:32], tops[j, 0, 0:32]], axis=0)
            res = res + dot(both, partner_pick[j])
        for q in range(2):
            for f in range(4):
                sign = -1.0 if f < 2 else 1.0
                part = sign * res[32 * q + 8 * f : 32 * q + 8 * f + 8]
                f_a[WIDE + count + q, f] = part[:, :128]
                f_b[WIDE + count + q, f] = part[:, 128:]

    def roots(r, _):
        k_a, k_b = f_a[r, 3], f_b[r, 3]
        e_a, e_b = east_of(k_a, k_b, lane)
        ks_a[r, 0] = jnp.sqrt(k_a * e_a)
        ks_b[r, 0] = jnp.sqrt(k_b * e_b)
        ks_a[r, 1] = jnp.sqrt(k_a * f_a[r + 1, 3])
        ks_b[r, 1] = jnp.sqrt(k_b * f_b[r + 1, 3])
        return 0

    lax.fori_loop(0, total - 1, roots, 0, unroll=2)

    def summed(x):
        for d in (1, 2, 4):
            x = x + jnp.where(level >= d, pltpu.roll(x, d, axis=0), 0.0)
        return x

    def step(src_a, src_b, dst_a, dst_b):
        def body(r, _):
            fr = coriolis[r]
            ke_a, ke_b = ks_a[r, 0], ks_b[r, 0]
            kw_a, kw_b = west_of(ke_a, ke_b, lane)
            coef = ((ke_a, kw_a, ks_a[r, 1], ks_a[r - 1, 1]), (ke_b, kw_b, ks_b[r, 1], ks_b[r - 1, 1]))
            mids, es, ws = [], [], []
            for f in range(3):
                a, b = src_a[r, f], src_b[r, f]
                mids.append((a, b))
                es.append(east_of(a, b, lane))
                ws.append(west_of(a, b, lane))
            for i, (src, dst, k_own) in enumerate(((src_a, dst_a, f_a[r, 3]), (src_b, dst_b, f_b[r, 3]))):
                wet = jnp.where(k_own > 0, 1.0, 0.0)
                ke, kw, kn, ks = coef[i]
                u, v, t = mids[0][i], mids[1][i], mids[2][i]
                ns = [src[r + 1, f] for f in range(3)]
                ss = [src[r - 1, f] for f in range(3)]
                outs = []
                for f in range(3):
                    m = mids[f][i]
                    outs.append(
                        m + ke * (es[f][i] - m) + kw * (ws[f][i] - m) + kn * (ns[f] - m) + ks * (ss[f] - m)
                    )
                dx = es[2][i] - ws[2][i]
                dy = ns[2] - ss[2]
                dst[r, 0] = wet * (outs[0] + fr * v - 0.025 * summed(dx))
                dst[r, 1] = wet * (outs[1] - fr * u - 0.025 * summed(dy))
                dst[r, 2] = wet * (outs[2] - 0.125 * (u * dx + v * dy))
            return 0

        return body

    lax.fori_loop(1, total - 1, step(f_a, f_b, h_a, h_b), 0, unroll=2)
    lax.fori_loop(2, total - 2, step(h_a, h_b, f_a, f_b), 0, unroll=2)

    lane24 = lax.broadcasted_iota(jnp.int32, (24, 128), 1)
    lane72 = lax.broadcasted_iota(jnp.int32, (72, 128), 1)
    pad8 = jnp.zeros((8, 128), F32)
    lines = []
    side = jnp.zeros((72, 128), F32)
    for q in range(count + 4):
        a = jnp.concatenate([f_a[q + 2, f] for f in range(3)], axis=0)
        b = jnp.concatenate([f_b[q + 2, f] for f in range(3)], axis=0)
        if q < 2:
            a, b = jnp.where(at_bottom, 0.0, a), jnp.where(at_bottom, 0.0, b)
        if q >= count + 2:
            a, b = jnp.where(at_top, 0.0, a), jnp.where(at_top, 0.0, b)
        e_a, e_b = east_of(a, b, lane24)
        w_a, w_b = west_of(a, b, lane24)
        lines.append(jnp.concatenate([w_a, a, e_a], axis=0))
        rim = jnp.concatenate([w_b, b, e_b], axis=0)
        side = jnp.where(lane72 // 2 == q, pltpu.roll(rim, (1 + 2 * q) % 128, axis=1), side)
        if q >= 2:
            r = q - 2
            patches[:, 128 * r : 128 * r + 128] = jnp.concatenate(lines[-3:] + [pad8], axis=0).astype(BF16)
    span = (count + 2) * 128
    patches[:, span : span + 128] = jnp.concatenate(
        [side, pltpu.roll(side, 126, axis=1), pltpu.roll(side, 124, axis=1), pad8], axis=0
    ).astype(BF16)
    patches[:, span + 128 :] = jnp.zeros((224, patches.shape[1] - span - 128), BF16)

    for start in range(0, patches.shape[1], 256):
        pre1 = dot(w_first[...], patches[:, start : start + 256])
        s1 = sigmoid(pre1)
        h1 = (pre1 * s1).astype(BF16)
        pre2 = dot(mix_w[...], h1)
        s2 = sigmoid(pre2)
        hid1[:, start : start + 256] = h1
        hid2[:, start : start + 256] = (pre2 * s2).astype(BF16).astype(F32)
        slope1[:, start : start + 256] = slope(pre1, s1)
        slope2[:, start : start + 256] = slope(pre2, s2)

    lane64 = lax.broadcasted_iota(jnp.int32, (64, 128), 1)
    lane16 = lax.broadcasted_iota(jnp.int32, (16, 128), 1)
    edge = hid2[:, span : span + 128]
    for r in range(count + 2):
        own = hid2[:, 128 * r : 128 * r + 128]
        to_w = jnp.where(lane64 == 0, pltpu.roll(edge, (128 - 2 * r) % 128, axis=1), pltpu.roll(own, 1, axis=1))
        to_e = jnp.where(lane64 == 127, pltpu.roll(edge, 126 - 2 * r, axis=1), pltpu.roll(own, 127, axis=1))
        both = jnp.concatenate([to_w, own, to_e], axis=0)
        if r == 0:
            both = jnp.where(at_bottom, 0.0, both)
        if r == count + 1:
            both = jnp.where(at_top, 0.0, both)
        hshift[:, 128 * r : 128 * r + 128] = both.astype(BF16)
    glines = []
    for r in range(count + 2):
        a, b = g_own[r, 0], g_own[r, 1]
        e_a, _ = east_of(a, b, lane16)
        w_a, _ = west_of(a, b, lane16)
        glines.append(jnp.concatenate([e_a, a, w_a], axis=0))
        if r >= 2:
            j = r - 2
            gpatch[:, 128 * j : 128 * j + 128] = jnp.concatenate(glines[-3:][::-1], axis=0).astype(BF16)

    cells = count * 128
    for start in range(0, cells, 256):
        here = slice(start, start + 256)
        near = slice(start + 128, start + 384)
        back = dot(w_back[...], gpatch[:, here])
        dm = (back * slope2[:, near]).astype(BF16)
        dmix[:, here] = dm
        dfirst[:, here] = (dot(w_mix_t[...], dm) * slope1[:, near]).astype(BF16)

    g_first = dot_cells(dfirst[...], patches[:, 128 : 128 + cells])
    g_mix = dot_cells(dmix[...], hid1[:, 128 : 128 + cells])
    g_mid = gpatch[64:80, :]
    g_last = jnp.concatenate([dot_cells(g_mid, hshift[:, 128 * i : 128 * i + cells]) for i in range(3)], axis=1)
    table[0:64, :] = g_first[:, :128]
    table[64:128, 0:96] = g_first[:, 128:224]
    table[64:128, 96:128] = jnp.zeros((64, 32), F32)
    table[128:192, 64:128] = jnp.zeros((64, 64), F32)
    table[128:192, 0:64] = g_mix
    table[128:144, 64:128] = g_last[:, 512:576]
    for i in range(4):
        table[192 + 16 * i : 208 + 16 * i, :] = g_last[:, 128 * i : 128 * i + 128]
    q = table[...].T
    hi = q.astype(BF16)
    lo = (q - hi.astype(F32)).astype(BF16)
    split = jnp.concatenate([hi, lo], axis=0)
    per = picked.shape[1]
    for j in range(0, krow.shape[0], 2):
        got = dot(split, picks[:, 128 * j : 128 * j + 256])
        got = got[:128] + got[128:]
        for i in range(2):
            mine = jnp.where(at_lane == klane[j + i : j + i + 1, :], got[:, 128 * i : 128 * i + 128], 0.0)
            to = (j + i) // per
            picked[to, (j + i) % per : (j + i) % per + 1, :] = jnp.sum(mine, axis=0, keepdims=True)

    lons = [lax.rem(lon + step, n_lon) for step in range(1, n_lon)]
    lats = [lax.rem(lat + step, n_lat) for step in range(1, n_lat)]
    def share(src, dst, ssem, rsem, to):
        return pltpu.make_async_remote_copy(
            src_ref=src, dst_ref=dst, send_sem=ssem, recv_sem=rsem, device_id=to, device_id_type=MESH
        )

    first = [share(picked.at[to], got_lon.at[lon], out_sem1.at[to], in_sem1.at[lon], (to, lat)) for to in lons]
    for c in first:
        c.start()
    got_lon[lon] = picked[lon]

    for start in range(0, cells, 256):
        tend = dot(w_last[0], hshift[:, start : start + 256])
        tend += dot(w_last[1], hshift[:, start + 128 : start + 384])
        tend += dot(w_last[2], hshift[:, start + 256 : start + 512])
        for j in range(2):
            r = start // 128 + j
            closing[:, r, :] = wet2s[r] * tend[:, 128 * j : 128 * j + 128]
    closure[...] = closing[...].astype(BF16)
    for row in range(count):
        for f in range(3):
            state[f, :, row, :] = f_a[row + WIDE, f]
    for c, to in zip(first, lons):
        c.wait_send()
        share(picked.at[to], got_lon.at[to], out_sem1.at[to], in_sem1.at[to], (to, lat)).wait_recv()
    got_lat[lat] = jnp.sum(got_lon[...], axis=0)
    second = [share(got_lat.at[lat], got_lat.at[lat], out_sem2.at[to], in_sem2.at[lat], (lon, to)) for to in lats]
    for c in second:
        c.start()
    for c, to in zip(second, lats):
        c.wait_send()
        share(got_lat.at[to], got_lat.at[to], out_sem2.at[to], in_sem2.at[to], (lon, to)).wait_recv()
    chunk[...] = jnp.sum(got_lat[...], axis=0)
    third = [share(chunk, out.at[lon], out_sem3.at[to], in_sem3.at[lon], (to, lat)) for to in lons]
    for c in third:
        c.start()
    out[lon] = chunk[...]
    for c, to in zip(third, lons):
        c.wait_send()
        share(chunk, out.at[to], out_sem3.at[to], in_sem3.at[to], (to, lat)).wait_recv()


def entry_place(index):
    k, rest = index // 1536, index % 1536
    col = (k * 24) + rest % 24
    row_f, lane_f = rest // 24 + 64 * (col // 128), col % 128
    m = index - 13824
    row_m, lane_m = 128 + m // 64, m % 64
    m = index - 17920
    o, col = (m % 1024) // 64, (m // 1024) * 64 + m % 64
    spill = col >= 512
    row_l = jnp.where(spill, 128 + o, 192 + 16 * (col // 128) + o)
    lane_l = jnp.where(spill, 64 + col - 512, col % 128)
    row = jnp.where(index < 13824, row_f, jnp.where(index < 17920, row_m, row_l))
    lane = jnp.where(index < 13824, lane_f, jnp.where(index < 17920, lane_m, lane_l))
    return row, lane


def on_device(
    n_lon, n_lat, ocean_state, diffusivity, depth_levels, fold_pair, first_weight, mix_weight, last_weight,
    cotangent, active_index,
):
    count = ocean_state.shape[2]
    row_total = count * n_lat
    scale = 1.0 / math.sqrt(row_total * 128 * n_lon)
    sds = jax.ShapeDtypeStruct
    dma = pltpu.SemaphoreType.DMA
    vmem = pltpu.VMEM
    row_ids = lax.axis_index("lat") * count - WIDE + jnp.arange(count + 2 * WIDE, dtype=jnp.int32)
    mirrored = jnp.where(row_ids >= row_total, 2 * row_total - 1 - row_ids, row_ids)
    rows_f = 0.25 * jnp.sin(math.pi * (mirrored.astype(F32) + 0.5) / row_total - 0.5 * math.pi)
    krow, klane = entry_place(active_index)
    picks = active_index.shape[0] // 128
    depth = picks // n_lon
    total = count + 2 * WIDE
    wide = (count + 4) * 128
    cells = count * 128
    state, closure, reduced = pl.pallas_call(
        functools.partial(kernel, n_lon, n_lat, scale),
        out_shape=[
            sds((3, 8, count, 128), F32), sds((16, count, 128), BF16), sds((n_lon, depth, 128), F32),
        ],
        in_specs=[SMEM] + [VMEM] * 9 + [SMEM],
        out_specs=[VMEM] * 3,
        scratch_shapes=[
            vmem((16, count, 128), F32), vmem((16, count, 128), F32),
            vmem((WIDE, 48, 128), BF16), vmem((WIDE, 48, 128), BF16), vmem((6, 48, 128), BF16),
            vmem((n_lon, 2, 48, 128), BF16), vmem((count, 48, 128), BF16), vmem((48, 128), BF16),
            vmem((n_lon, 128, 256), BF16), vmem((256, picks * 128), BF16),
            vmem((64, 224), BF16), vmem((3, 16, 192), BF16), vmem((64, 144), BF16), vmem((64, 64), BF16),
            vmem((total, 4, 8, 128), F32), vmem((total, 4, 8, 128), F32),
            vmem((total, 3, 8, 128), F32), vmem((total, 3, 8, 128), F32),
            vmem((total, 2, 8, 128), F32), vmem((total, 2, 8, 128), F32),
            vmem((count + 2, 2, 16, 128), F32), vmem((count, 16, 128), F32),
            vmem((224, wide), BF16), vmem((64, wide), F32), vmem((64, wide), F32),
            vmem((64, wide), BF16), vmem((64, wide), F32), vmem((192, (count + 2) * 128), BF16),
            vmem((144, cells), BF16), vmem((64, cells), BF16), vmem((64, cells), BF16),
            vmem((256, 128), F32),
            vmem((n_lon, depth, 128), F32), vmem((n_lon, depth, 128), F32), vmem((n_lat, depth, 128), F32),
            vmem((depth, 128), F32),
            dma((2,)), dma((2,)), dma((6,)), dma((6,)), dma((n_lon,)), dma((n_lon,)),
            dma((n_lon,)), dma((n_lon,)), dma((n_lat,)), dma((n_lat,)), dma((n_lon,)), dma((n_lon,)),
        ],
        compiler_params=pltpu.CompilerParams(
            collective_id=0, has_side_effects=True, vmem_limit_bytes=48 * 1024 * 1024
        ),
        name="ocean",
    )(
        fold_pair, ocean_state, diffusivity, depth_levels, cotangent, first_weight, mix_weight, last_weight,
        krow.reshape(picks, 128), klane.reshape(picks, 128), rows_f,
    )
    return state, closure, reduced.reshape(-1)


def solution(mesh):
    in_specs = (
        P(None, None, "lat", "lon"), P(None, "lat", "lon"), P("lat", "lon"), P(), P(), P(), P(),
        P(None, "lat", "lon"), P(),
    )
    out_specs = (P(None, None, "lat", "lon"), P(None, "lat", "lon"), P())
    return jax.shard_map(
        functools.partial(on_device, mesh.shape["lon"], mesh.shape["lat"]),
        mesh=mesh, in_specs=in_specs, out_specs=out_specs, check_vma=False,
    )
```

```python
import functools
import math

import jax
import jax.numpy as jnp
from jax import lax
from jax.experimental import pallas as pl
from jax.experimental.pallas import tpu as pltpu
from jax.sharding import PartitionSpec as P

MESH = pl.DeviceIdType.MESH
F32 = jnp.float32
BF16 = jnp.bfloat16
WIDE = 4
VMEM = pl.BlockSpec(memory_space=pltpu.VMEM)
HBM = pl.BlockSpec(memory_space=pltpu.HBM)
ANY = pl.BlockSpec(memory_space=pl.ANY)


def masked_row(ocean, kappa, depth, cot, row, scale):
    levels = lax.broadcasted_iota(jnp.int32, (8, 128), 0)
    wet = (levels < depth[pl.ds(row, 1), :]).astype(F32)
    u = ocean[0, :, row, :] * wet
    v = ocean[1, :, row, :] * wet
    t = ocean[2, :, row, :] * wet
    k = kappa[:, row, :] * wet
    wet2 = jnp.concatenate([wet, wet], axis=0)
    g = scale * wet2 * cot[:, row, :]
    return u, v, t, k, g, wet2


def dot(a, b):
    return jnp.dot(a, b, preferred_element_type=F32)


def dot_cells(a, b):
    return lax.dot_general(a, b, (((1,), (1,)), ((), ())), preferred_element_type=F32)


def dot_first(a, b):
    return lax.dot_general(a, b, (((0,), (0,)), ((), ())), preferred_element_type=F32)


def slope(pre, sigma):
    return sigma * (1.0 + pre * (1.0 - sigma))


def sigmoid(pre):
    return 0.5 + 0.5 * jnp.tanh(0.5 * pre)


def east_of(own, rim, lane):
    a = pltpu.roll(own, 127, axis=own.ndim - 1)
    b = pltpu.roll(rim, 127, axis=own.ndim - 1)
    return jnp.where(lane == 127, b, a), jnp.where(lane == 127, a, b)


def west_of(own, rim, lane):
    a = pltpu.roll(own, 1, axis=own.ndim - 1)
    b = pltpu.roll(rim, 1, axis=own.ndim - 1)
    return jnp.where(lane == 0, b, a), jnp.where(lane == 0, a, b)


def kernel(
    n_lon, n_lat, scale, *refs,
):
    operands, refs = refs[:9], refs[9:]
    outputs, refs = refs[:3], refs[3:]
    held, refs = refs[:9], refs[9:]
    loads = [pltpu.make_async_copy(a, b, refs[0].at[i]) for i, (a, b) in enumerate(zip(operands, held))]
    for i in (0, 1, 2, 3, 5, 6, 7, 8, 4):
        loads[i].start()
    ocean_step(n_lon, n_lat, scale, loads, *held, *outputs, *refs[1:])


def ocean_step(
    n_lon, n_lat, scale, loads, ocean, kappa, depth, cot_in, fold, first_w, mix_w, last_w, active,
    state, closure, out,
    krow, klane, coriolis, north_g, south_g, cot, closing, north, south, sides, tops, rows, packed, partner_pick, picks, w_first, w_last, w_back, w_mix_t,
    f_a, f_b, h_a, h_b, ks_a, ks_b, g_own, wet2s, patches, slope1, slope2, hid1, hid2, hshift, gpatch, dmix, dfirst, table,
    picked, got_lon, got_lat, chunk,
    row_send, row_recv, g_send, g_recv, side_send, side_recv, top_send, top_recv, out_sem1, in_sem1, out_sem2, in_sem2, out_sem3, in_sem3,
):
    lon = lax.axis_index("lon")
    lat = lax.axis_index("lat")
    count = rows.shape[0]
    east = lax.rem(lon + 1, n_lon)
    west = lax.rem(lon + n_lon - 1, n_lon)
    has_north = lat < n_lat - 1
    has_south = lat > 0
    at_top = lat == n_lat - 1

    barrier = pltpu.get_barrier_semaphore()

    def greet(to_lat, to_lon):
        pl.semaphore_signal(barrier, inc=1, device_id=(to_lon, to_lat), device_id_type=MESH)

    for step in range(1, n_lon):
        greet(lat, lax.rem(lon + step, n_lon))
    for step in range(1, n_lat):
        greet(lax.rem(lat + step, n_lat), lon)

    @pl.when(has_north)
    def _():
        for to in (east, west):
            greet(lat + 1, to)

    @pl.when(has_south)
    def _():
        for to in (east, west):
            greet(lat - 1, to)

    for load in loads[:4]:
        load.wait()
    cot[...] = cot_in[...].astype(F32)
    lanes = lax.broadcasted_iota(jnp.int32, (48, 128), 1)
    acc = jnp.zeros((48, 128), F32)
    for row in range(count):
        u, v, t, k, g, wet2 = masked_row(ocean, kappa, depth, cot, row, scale)
        line = jnp.concatenate([u, v, t, k, g], axis=0)
        for f, field in enumerate((u, v, t, k)):
            f_a[row + WIDE, f] = field
        g_own[row + 1, 0] = g.astype(BF16).astype(F32)
        wet2s[row] = wet2
        rows[row] = line.astype(BF16)
        acc = jnp.where(lanes // 8 == row, pltpu.roll(line, (4 + 8 * row) % 128, axis=1), acc)
    packed[...] = acc.astype(BF16)

    sides_open = has_north.astype(jnp.int32) + has_south.astype(jnp.int32)
    pl.semaphore_wait(barrier, n_lon + n_lat - 2 + 2 * sides_open)

    def send_rows(start, dst, slot, to_lat):
        return pltpu.make_async_remote_copy(
            src_ref=rows.at[pl.ds(start, WIDE), pl.ds(0, 32)], dst_ref=dst, send_sem=row_send.at[slot],
            recv_sem=row_recv.at[slot], device_id=(lon, to_lat), device_id_type=MESH,
        )

    def send_g(start, dst, slot, to_lat):
        return pltpu.make_async_remote_copy(
            src_ref=rows.at[start, pl.ds(32, 16)], dst_ref=dst, send_sem=g_send.at[slot],
            recv_sem=g_recv.at[slot], device_id=(lon, to_lat), device_id_type=MESH,
        )

    def send_side(slot, to_lat, to_lon):
        return pltpu.make_async_remote_copy(
            src_ref=packed, dst_ref=sides.at[slot], send_sem=side_send.at[slot],
            recv_sem=side_recv.at[slot], device_id=(to_lon, to_lat), device_id_type=MESH,
        )

    def send_top(step):
        return pltpu.make_async_remote_copy(
            src_ref=rows.at[pl.ds(count - 2, 2), pl.ds(0, 32)], dst_ref=tops.at[lon], send_sem=top_send.at[step],
            recv_sem=top_recv.at[lon], device_id=(lax.rem(lon + step, n_lon), lat), device_id_type=MESH,
        )

    def top_from(step):
        peer = lax.rem(lon + step, n_lon)
        return pltpu.make_async_remote_copy(
            src_ref=rows.at[pl.ds(count - 2, 2), pl.ds(0, 32)], dst_ref=tops.at[peer], send_sem=top_send.at[step],
            recv_sem=top_recv.at[peer], device_id=(peer, lat), device_id_type=MESH,
        )

    to_north = send_rows(count - WIDE, south, 0, lat + 1)
    to_south = send_rows(0, north, 1, lat - 1)
    g_north = send_g(count - 1, south_g, 0, lat + 1)
    g_south = send_g(0, north_g, 1, lat - 1)
    same = [send_side(0, lat, east), send_side(1, lat, west)]
    up = [send_side(2, lat + 1, east), send_side(3, lat + 1, west)]
    down = [send_side(4, lat - 1, east), send_side(5, lat - 1, west)]

    for copy in same:
        copy.start()

    @pl.when(at_top)
    def _():
        for step in range(1, n_lon):
            send_top(step).start()

    @pl.when(has_north)
    def _():
        to_north.start()

    @pl.when(has_south)
    def _():
        to_south.start()

    @pl.when(has_north)
    def _():
        for copy in up:
            copy.start()
        g_north.start()

    @pl.when(has_south)
    def _():
        for copy in down:
            copy.start()
        g_south.start()


    def placed(height, width, shift):
        at = lax.broadcasted_iota(jnp.int32, (height, width), 0)
        to = lax.broadcasted_iota(jnp.int32, (height, width), 1)
        return jnp.where(at + shift == to, 1.0, 0.0).astype(BF16)

    for load in loads[4:]:
        load.wait()
    first = lat * count - WIDE
    row_total = count * n_lat
    row_ids = first + lax.broadcasted_iota(jnp.int32, coriolis.shape, 0)
    mirrored = jnp.where(row_ids >= row_total, 2 * row_total - 1 - row_ids, row_ids)
    coriolis[...] = 0.25 * jnp.sin(math.pi * (mirrored.astype(F32) + 0.5) / row_total - 0.5 * math.pi)
    krow[...], klane[...] = entry_place(active[...])
    wide_w = dot_first(first_w[0], placed(24, 224, 0))
    for k in range(1, 9):
        wide_w += dot_first(first_w[k], placed(24, 224, 24 * k))
    w_first[...] = wide_w.astype(BF16)
    for k in range(3):
        w_last[k] = sum(dot(last_w[3 * k + i], placed(64, 192, 64 * i)) for i in range(3)).astype(BF16)
    back_w = jnp.concatenate([last_w[k].astype(F32) for k in range(9)], axis=0)
    w_back[...] = back_w.T.astype(BF16)
    w_mix_t[...] = mix_w[...].astype(F32).T.astype(BF16)
    at_row = lax.broadcasted_iota(jnp.int32, (256, 128), 0)
    at_lane = lax.broadcasted_iota(jnp.int32, (128, 128), 0)
    for j in range(krow.shape[0]):
        picks[:, 128 * j : 128 * j + 128] = jnp.where(at_row == krow[j : j + 1, :], 1.0, 0.0).astype(BF16)

    @pl.when(at_top)
    def _():
        nx = n_lon * 128
        s = fold[0:1, 0:1]
        at = lax.broadcasted_iota(jnp.int32, (128, 256), 0)
        pos = lax.broadcasted_iota(jnp.int32, (1, 256), 1)
        col = lon * 128 + jnp.where(pos >= 192, pos - 256, pos)
        col = jnp.where(col < 0, col + nx, col)
        col = jnp.where(col >= nx, col - nx, col)
        partner = s - col
        partner = jnp.where(partner < 0, partner + nx, partner)
        for j in range(n_lon):
            partner_pick[j] = jnp.where(at + 128 * j == partner, 1.0, 0.0).astype(BF16)

    total = count + 2 * WIDE
    at_bottom = lat == 0
    lane = lax.broadcasted_iota(jnp.int32, (8, 128), 1)
    level = lax.broadcasted_iota(jnp.int32, (8, 128), 0)
    lane48 = lax.broadcasted_iota(jnp.int32, (48, 128), 1)
    zero32 = jnp.zeros((32, 128), F32)
    zero48 = jnp.zeros((48, 128), F32)

    def merge(low):
        odd = lane48 % 8 >= 4
        return jnp.where(odd, sides[low + 1].astype(F32), sides[low].astype(F32))

    def put(row, own, rim):
        for f in range(4):
            if own is not None:
                f_a[row, f] = own[8 * f : 8 * f + 8]
            f_b[row, f] = rim[8 * f : 8 * f + 8]
        if WIDE - 1 <= row <= WIDE + count:
            g_own[row - WIDE + 1, 1] = rim[32:48]

    def unpack(side, row):
        return pltpu.roll(side, (128 - 4 - 8 * row) % 128, axis=1)

    def roots(r, _):
        k_a, k_b = f_a[r, 3], f_b[r, 3]
        e_a, e_b = east_of(k_a, k_b, lane)
        ks_a[r, 0] = jnp.sqrt(k_a * e_a)
        ks_b[r, 0] = jnp.sqrt(k_b * e_b)
        ks_a[r, 1] = jnp.sqrt(k_a * f_a[r + 1, 3])
        ks_b[r, 1] = jnp.sqrt(k_b * f_b[r + 1, 3])
        return 0

    def summed(x):
        for d in (1, 2, 4):
            x = x + jnp.where(level >= d, pltpu.roll(x, d, axis=0), 0.0)
        return x

    def step(src_a, src_b, dst_a, dst_b):
        def body(r, _):
            fr = coriolis[pl.ds(r, 1), :]
            ke_a, ke_b = ks_a[r, 0], ks_b[r, 0]
            kw_a, kw_b = west_of(ke_a, ke_b, lane)
            coef = ((ke_a, kw_a, ks_a[r, 1], ks_a[r - 1, 1]), (ke_b, kw_b, ks_b[r, 1], ks_b[r - 1, 1]))
            mids, es, ws = [], [], []
            for f in range(3):
                a, b = src_a[r, f], src_b[r, f]
                mids.append((a, b))
                es.append(east_of(a, b, lane))
                ws.append(west_of(a, b, lane))
            for i, (src, dst, k_own) in enumerate(((src_a, dst_a, f_a[r, 3]), (src_b, dst_b, f_b[r, 3]))):
                wet = jnp.where(k_own > 0, 1.0, 0.0)
                ke, kw, kn, ks = coef[i]
                u, v, t = mids[0][i], mids[1][i], mids[2][i]
                ns = [src[r + 1, f] for f in range(3)]
                ss = [src[r - 1, f] for f in range(3)]
                outs = []
                for f in range(3):
                    m = mids[f][i]
                    outs.append(
                        m + ke * (es[f][i] - m) + kw * (ws[f][i] - m) + kn * (ns[f] - m) + ks * (ss[f] - m)
                    )
                dx = es[2][i] - ws[2][i]
                dy = ns[2] - ss[2]
                dst[r, 0] = wet * (outs[0] + fr * v - 0.025 * summed(dx))
                dst[r, 1] = wet * (outs[1] - fr * u - 0.025 * summed(dy))
                dst[r, 2] = wet * (outs[2] - 0.125 * (u * dx + v * dy))
            return 0

        return body

    first_step = step(f_a, f_b, h_a, h_b)
    for copy in same:
        copy.wait()
    mid = merge(0)
    for row in range(count):
        put(row + WIDE, None, unpack(mid, row))
    low, high = WIDE, WIDE + count - 1
    lax.fori_loop(low, high, roots, 0, unroll=3)
    lax.fori_loop(low + 1, high, first_step, 0, unroll=2)

    @pl.when(has_north)
    def _():
        to_north.wait_send()
        to_south.wait_recv()
        g_north.wait_send()
        g_south.wait_recv()
        for copy in up:
            copy.wait_send()
        for copy in down:
            copy.wait_recv()

    @pl.when(has_south)
    def _():
        to_south.wait_send()
        to_north.wait_recv()
        g_south.wait_send()
        g_north.wait_recv()
        for copy in down:
            copy.wait_send()
        for copy in up:
            copy.wait_recv()

    @pl.when(at_top)
    def _():
        tops[lon] = rows[count - 2 : count, 0:32]
        for step in range(1, n_lon):
            send_top(step).wait_send()
            top_from(step).wait_recv()

    below = jnp.where(at_bottom, zero48, merge(2))
    above = jnp.where(at_top, zero48, merge(4))
    for row in range(WIDE):
        put(row, jnp.where(at_bottom, zero32, south[row].astype(F32)), unpack(below, count - WIDE + row))
        put(WIDE + count + row, jnp.where(at_top, zero32, north[row].astype(F32)), unpack(above, row))

    g_own[0, 0] = jnp.where(at_bottom, zero48[:16], south_g[...].astype(F32))
    g_own[count + 1, 0] = jnp.where(at_top, zero48[:16], north_g[...].astype(F32))

    @pl.when(at_top)
    def _():
        res = jnp.zeros((64, 256), F32)
        for j in range(n_lon):
            both = jnp.concatenate([tops[j, 1, 0:32], tops[j, 0, 0:32]], axis=0)
            res = res + dot(both, partner_pick[j])
        for q in range(2):
            for f in range(4):
                sign = -1.0 if f < 2 else 1.0
                part = sign * res[32 * q + 8 * f : 32 * q + 8 * f + 8]
                f_a[WIDE + count + q, f] = part[:, :128]
                f_b[WIDE + count + q, f] = part[:, 128:]

    lax.fori_loop(0, low, roots, 0, unroll=True)
    lax.fori_loop(high, total - 1, roots, 0, unroll=True)
    lax.fori_loop(1, low + 1, first_step, 0, unroll=2)
    lax.fori_loop(high, total - 1, first_step, 0, unroll=2)
    lax.fori_loop(2, total - 2, step(h_a, h_b, f_a, f_b), 0, unroll=2)

    lane24 = lax.broadcasted_iota(jnp.int32, (24, 128), 1)
    lane72 = lax.broadcasted_iota(jnp.int32, (72, 128), 1)
    pad8 = jnp.zeros((8, 128), F32)
    lines = []
    side = jnp.zeros((72, 128), F32)
    for q in range(count + 4):
        a = jnp.concatenate([f_a[q + 2, f] for f in range(3)], axis=0)
        b = jnp.concatenate([f_b[q + 2, f] for f in range(3)], axis=0)
        if q < 2:
            a, b = jnp.where(at_bottom, 0.0, a), jnp.where(at_bottom, 0.0, b)
        if q >= count + 2:
            a, b = jnp.where(at_top, 0.0, a), jnp.where(at_top, 0.0, b)
        e_a, e_b = east_of(a, b, lane24)
        w_a, w_b = west_of(a, b, lane24)
        lines.append(jnp.concatenate([w_a, a, e_a], axis=0))
        rim = jnp.concatenate([w_b, b, e_b], axis=0)
        side = jnp.where(lane72 // 2 == q, pltpu.roll(rim, (1 + 2 * q) % 128, axis=1), side)
        if q >= 2:
            r = q - 2
            patches[:, 128 * r : 128 * r + 128] = jnp.concatenate(lines[-3:] + [pad8], axis=0).astype(BF16)
    span = (count + 2) * 128
    patches[:, span : span + 128] = jnp.concatenate(
        [side, pltpu.roll(side, 126, axis=1), pltpu.roll(side, 124, axis=1), pad8], axis=0
    ).astype(BF16)
    patches[:, span + 128 :] = jnp.zeros((224, patches.shape[1] - span - 128), BF16)

    for start in range(0, patches.shape[1], 256):
        pre1 = dot(w_first[...], patches[:, start : start + 256])
        s1 = sigmoid(pre1)
        h1 = (pre1 * s1).astype(BF16)
        pre2 = dot(mix_w[...], h1)
        s2 = sigmoid(pre2)
        hid1[:, start : start + 256] = h1
        hid2[:, start : start + 256] = (pre2 * s2).astype(BF16).astype(F32)
        slope1[:, start : start + 256] = slope(pre1, s1)
        slope2[:, start : start + 256] = slope(pre2, s2)

    lane64 = lax.broadcasted_iota(jnp.int32, (64, 128), 1)
    lane16 = lax.broadcasted_iota(jnp.int32, (16, 128), 1)
    edge = hid2[:, span : span + 128]
    for r in range(count + 2):
        own = hid2[:, 128 * r : 128 * r + 128]
        to_w = jnp.where(lane64 == 0, pltpu.roll(edge, (128 - 2 * r) % 128, axis=1), pltpu.roll(own, 1, axis=1))
        to_e = jnp.where(lane64 == 127, pltpu.roll(edge, 126 - 2 * r, axis=1), pltpu.roll(own, 127, axis=1))
        both = jnp.concatenate([to_w, own, to_e], axis=0)
        if r == 0:
            both = jnp.where(at_bottom, 0.0, both)
        if r == count + 1:
            both = jnp.where(at_top, 0.0, both)
        hshift[:, 128 * r : 128 * r + 128] = both.astype(BF16)
    glines = []
    for r in range(count + 2):
        a, b = g_own[r, 0], g_own[r, 1]
        e_a, _ = east_of(a, b, lane16)
        w_a, _ = west_of(a, b, lane16)
        glines.append(jnp.concatenate([e_a, a, w_a], axis=0))
        if r >= 2:
            j = r - 2
            gpatch[:, 128 * j : 128 * j + 128] = jnp.concatenate(glines[-3:][::-1], axis=0).astype(BF16)

    cells = count * 128
    for start in range(0, cells, 256):
        here = slice(start, start + 256)
        near = slice(start + 128, start + 384)
        back = dot(w_back[...], gpatch[:, here])
        dm = (back * slope2[:, near]).astype(BF16)
        dmix[:, here] = dm
        dfirst[:, here] = (dot(w_mix_t[...], dm) * slope1[:, near]).astype(BF16)

    g_first = dot_cells(dfirst[...], patches[:, 128 : 128 + cells])
    g_mix = dot_cells(dmix[...], hid1[:, 128 : 128 + cells])
    g_mid = gpatch[64:80, :]
    g_last = jnp.concatenate([dot_cells(g_mid, hshift[:, 128 * i : 128 * i + cells]) for i in range(3)], axis=1)
    table[0:64, :] = g_first[:, :128]
    table[64:128, 0:96] = g_first[:, 128:224]
    table[64:128, 96:128] = jnp.zeros((64, 32), F32)
    table[128:192, 64:128] = jnp.zeros((64, 64), F32)
    table[128:192, 0:64] = g_mix
    table[128:144, 64:128] = g_last[:, 512:576]
    for i in range(4):
        table[192 + 16 * i : 208 + 16 * i, :] = g_last[:, 128 * i : 128 * i + 128]
    q = table[...].T
    hi = q.astype(BF16)
    lo = (q - hi.astype(F32)).astype(BF16)
    split = jnp.concatenate([hi, lo], axis=0)
    per = picked.shape[1]
    for j in range(0, krow.shape[0], 2):
        got = dot(split, picks[:, 128 * j : 128 * j + 256])
        got = got[:128] + got[128:]
        for i in range(2):
            mine = jnp.where(at_lane == klane[j + i : j + i + 1, :], got[:, 128 * i : 128 * i + 128], 0.0)
            to = (j + i) // per
            picked[to, (j + i) % per : (j + i) % per + 1, :] = jnp.sum(mine, axis=0, keepdims=True)

    lons = [lax.rem(lon + step, n_lon) for step in range(1, n_lon)]
    lats = [lax.rem(lat + step, n_lat) for step in range(1, n_lat)]
    def share(src, dst, ssem, rsem, to):
        return pltpu.make_async_remote_copy(
            src_ref=src, dst_ref=dst, send_sem=ssem, recv_sem=rsem, device_id=to, device_id_type=MESH
        )

    first = [share(picked.at[to], got_lon.at[lon], out_sem1.at[to], in_sem1.at[lon], (to, lat)) for to in lons]
    for c in first:
        c.start()
    got_lon[lon] = picked[lon]

    for start in range(0, cells, 256):
        tend = dot(w_last[0], hshift[:, start : start + 256])
        tend += dot(w_last[1], hshift[:, start + 128 : start + 384])
        tend += dot(w_last[2], hshift[:, start + 256 : start + 512])
        for j in range(2):
            r = start // 128 + j
            closing[:, r, :] = wet2s[r] * tend[:, 128 * j : 128 * j + 128]
    closure[...] = closing[...].astype(BF16)
    for row in range(count):
        for f in range(3):
            state[f, :, row, :] = f_a[row + WIDE, f]
    for c, to in zip(first, lons):
        c.wait_send()
        share(picked.at[to], got_lon.at[to], out_sem1.at[to], in_sem1.at[to], (to, lat)).wait_recv()
    got_lat[lat] = jnp.sum(got_lon[...], axis=0)
    second = [share(got_lat.at[lat], got_lat.at[lat], out_sem2.at[to], in_sem2.at[lat], (lon, to)) for to in lats]
    for c in second:
        c.start()
    for c, to in zip(second, lats):
        c.wait_send()
        share(got_lat.at[to], got_lat.at[to], out_sem2.at[to], in_sem2.at[to], (lon, to)).wait_recv()
    chunk[...] = jnp.sum(got_lat[...], axis=0)
    third = [share(chunk, out.at[lon], out_sem3.at[to], in_sem3.at[lon], (to, lat)) for to in lons]
    for c in third:
        c.start()
    out[lon] = chunk[...]
    for c, to in zip(third, lons):
        c.wait_send()
        share(chunk, out.at[to], out_sem3.at[to], in_sem3.at[to], (to, lat)).wait_recv()


def entry_place(index):
    def parts(value, size):
        whole = jnp.floor((value.astype(F32) + 0.5) * (1.0 / size)).astype(jnp.int32)
        return whole, value - size * whole

    k, rest = parts(index, 1536)
    o, c = parts(rest, 24)
    col = k * 24 + c
    row_f, lane_f = o + 64 * (col >> 7), col & 127
    m = index - 13824
    row_m, lane_m = 128 + (m >> 6), m & 63
    m = index - 17920
    o, col = (m & 1023) >> 6, (m >> 10) * 64 + (m & 63)
    spill = col >= 512
    row_l = jnp.where(spill, 128 + o, 192 + 16 * (col >> 7) + o)
    lane_l = jnp.where(spill, 64 + col - 512, col & 127)
    row = jnp.where(index < 13824, row_f, jnp.where(index < 17920, row_m, row_l))
    lane = jnp.where(index < 13824, lane_f, jnp.where(index < 17920, lane_m, lane_l))
    return row, lane


def store_kernel(*refs):
    copies = [pltpu.make_async_copy(refs[i], refs[3 + i], refs[6].at[i]) for i in range(3)]
    for copy in copies:
        copy.start()
    for copy in copies:
        copy.wait()


def on_device(
    n_lon, n_lat, ocean_state, diffusivity, depth_levels, fold_pair, first_weight, mix_weight, last_weight,
    cotangent, active_index,
):
    count = ocean_state.shape[2]
    row_total = count * n_lat
    scale = 1.0 / math.sqrt(row_total * 128 * n_lon)
    sds = jax.ShapeDtypeStruct
    dma = pltpu.SemaphoreType.DMA
    vmem = pltpu.VMEM
    picks = active_index.shape[0] // 128
    depth = picks // n_lon
    total = count + 2 * WIDE
    wide = (count + 4) * 128
    cells = count * 128
    operands = (
        ocean_state, diffusivity, depth_levels, cotangent, fold_pair.reshape(-1, 128),
        jnp.transpose(first_weight, (0, 2, 1)), mix_weight, last_weight, active_index.reshape(picks, 128),
    )
    outs = [
        sds((3, 8, count, 128), F32), sds((16, count, 128), BF16), sds((n_lon, depth, 128), F32),
    ]
    results = pl.pallas_call(
        functools.partial(kernel, n_lon, n_lat, scale),
        out_shape=outs,
        in_specs=[HBM] * 9,
        out_specs=[VMEM] * 3,
        scratch_shapes=[vmem(x.shape, x.dtype) for x in operands] + [
            dma((9,)), vmem((picks, 128), jnp.int32), vmem((picks, 128), jnp.int32), vmem((total, 128), F32),
            vmem((16, 128), BF16), vmem((16, 128), BF16),
            vmem((16, count, 128), F32), vmem((16, count, 128), F32),
            vmem((WIDE, 32, 128), BF16), vmem((WIDE, 32, 128), BF16), vmem((6, 48, 128), BF16),
            vmem((n_lon, 2, 32, 128), BF16), vmem((count, 48, 128), BF16), vmem((48, 128), BF16),
            vmem((n_lon, 128, 256), BF16), vmem((256, picks * 128), BF16),
            vmem((64, 224), BF16), vmem((3, 16, 192), BF16), vmem((64, 144), BF16), vmem((64, 64), BF16),
            vmem((total, 4, 8, 128), F32), vmem((total, 4, 8, 128), F32),
            vmem((total, 3, 8, 128), F32), vmem((total, 3, 8, 128), F32),
            vmem((total, 2, 8, 128), F32), vmem((total, 2, 8, 128), F32),
            vmem((count + 2, 2, 16, 128), F32), vmem((count, 16, 128), F32),
            vmem((224, wide), BF16), vmem((64, wide), F32), vmem((64, wide), F32),
            vmem((64, wide), BF16), vmem((64, wide), F32), vmem((192, (count + 2) * 128), BF16),
            vmem((144, cells), BF16), vmem((64, cells), BF16), vmem((64, cells), BF16),
            vmem((256, 128), F32),
            vmem((n_lon, depth, 128), F32), vmem((n_lon, depth, 128), F32), vmem((n_lat, depth, 128), F32),
            vmem((depth, 128), F32),
            dma((2,)), dma((2,)), dma((2,)), dma((2,)), dma((6,)), dma((6,)), dma((n_lon,)), dma((n_lon,)),
            dma((n_lon,)), dma((n_lon,)), dma((n_lat,)), dma((n_lat,)), dma((n_lon,)), dma((n_lon,)),
        ],
        compiler_params=pltpu.CompilerParams(
            collective_id=0, has_side_effects=True, vmem_limit_bytes=48 * 1024 * 1024
        ),
        name="ocean",
    )(*operands)
    state, closure, reduced = pl.pallas_call(
        store_kernel,
        out_shape=outs,
        in_specs=[ANY] * 3,
        out_specs=[ANY] * 3,
        scratch_shapes=[dma((3,))],
        name="store",
    )(*results)
    return state, closure, reduced.reshape(-1)


def solution(mesh):
    in_specs = (
        P(None, None, "lat", "lon"), P(None, "lat", "lon"), P("lat", "lon"), P(), P(), P(), P(),
        P(None, "lat", "lon"), P(),
    )
    out_specs = (P(None, None, "lat", "lon"), P(None, "lat", "lon"), P())
    return jax.shard_map(
        functools.partial(on_device, mesh.shape["lon"], mesh.shape["lat"]),
        mesh=mesh, in_specs=in_specs, out_specs=out_specs, check_vma=False,
    )
```

```python
import functools
import math

import jax
import jax.numpy as jnp
from jax import lax
from jax.experimental import pallas as pl
from jax.experimental.pallas import tpu as pltpu
from jax.sharding import PartitionSpec as P

MESH = pl.DeviceIdType.MESH
F32 = jnp.float32
BF16 = jnp.bfloat16
GRANT = 62 * 1024 * 1024
WIDE = 4
HBM = pl.BlockSpec(memory_space=pltpu.HBM)
ANY = pl.BlockSpec(memory_space=pl.ANY)


def masked_row(ocean, kappa, depth, cot, row, scale):
    levels = lax.broadcasted_iota(jnp.int32, (8, 128), 0)
    wet = (levels < depth[pl.ds(row, 1), :]).astype(F32)
    u = ocean[0, :, row, :] * wet
    v = ocean[1, :, row, :] * wet
    t = ocean[2, :, row, :] * wet
    k = kappa[:, row, :] * wet
    wet2 = jnp.concatenate([wet, wet], axis=0)
    g = scale * wet2 * cot[:, row, :]
    return u, v, t, k, g, wet2


def dot(a, b):
    return jnp.dot(a, b, preferred_element_type=F32)


def dot_cells(a, b):
    return lax.dot_general(a, b, (((1,), (1,)), ((), ())), preferred_element_type=F32)


def dot_first(a, b):
    return lax.dot_general(a, b, (((0,), (0,)), ((), ())), preferred_element_type=F32)


def slope(pre, sigma):
    return sigma * (1.0 + pre * (1.0 - sigma))


def sigmoid(pre):
    return 0.5 + 0.5 * jnp.tanh(0.5 * pre)


def east_of(own, rim, lane):
    a = pltpu.roll(own, 127, axis=own.ndim - 1)
    b = pltpu.roll(rim, 127, axis=own.ndim - 1)
    return jnp.where(lane == 127, b, a), jnp.where(lane == 127, a, b)


def west_of(own, rim, lane):
    a = pltpu.roll(own, 1, axis=own.ndim - 1)
    b = pltpu.roll(rim, 1, axis=own.ndim - 1)
    return jnp.where(lane == 0, b, a), jnp.where(lane == 0, a, b)


def kernel(
    n_lon, n_lat, scale, *refs,
):
    operands, refs = refs[:9], refs[9:]
    outputs, refs = refs[:3], refs[3:]
    held, refs = refs[:9], refs[9:]
    loads = [pltpu.make_async_copy(a, b, refs[0].at[i]) for i, (a, b) in enumerate(zip(operands, held))]
    for i in (0, 1, 2, 3, 5, 6, 7, 8, 4):
        loads[i].start()
    ocean_step(n_lon, n_lat, scale, loads, *held, *outputs, *refs[1:])


def ocean_step(
    n_lon, n_lat, scale, loads, ocean, kappa, depth, cot_in, fold, first_w, mix_w, last_w, active,
    state, closure, out,
    krow, klane, coriolis, north_g, south_g, cot, closing, north, south, sides, tops, rows, packed, partner_pick, picks, w_first, w_last, w_back, w_mix_t,
    f_a, f_b, h_a, h_b, ks_a, ks_b, g_own, wet2s, patches, slope1, slope2, hid1, hid2, hshift, gpatch, dmix, dfirst, table,
    picked, got_lon, got_lat, chunk, state_out, closure_out, out_sem,
    row_send, row_recv, g_send, g_recv, side_send, side_recv, top_send, top_recv, out_sem1, in_sem1, out_sem2, in_sem2, out_sem3, in_sem3,
):
    lon = lax.axis_index("lon")
    lat = lax.axis_index("lat")
    count = rows.shape[0]
    east = lax.rem(lon + 1, n_lon)
    west = lax.rem(lon + n_lon - 1, n_lon)
    has_north = lat < n_lat - 1
    has_south = lat > 0
    at_top = lat == n_lat - 1

    barrier = pltpu.get_barrier_semaphore()

    def greet(to_lat, to_lon):
        pl.semaphore_signal(barrier, inc=1, device_id=(to_lon, to_lat), device_id_type=MESH)

    for step in range(1, n_lon):
        greet(lat, lax.rem(lon + step, n_lon))
    for step in range(1, n_lat):
        greet(lax.rem(lat + step, n_lat), lon)

    @pl.when(has_north)
    def _():
        for to in (east, west):
            greet(lat + 1, to)

    @pl.when(has_south)
    def _():
        for to in (east, west):
            greet(lat - 1, to)

    for load in loads[:4]:
        load.wait()
    cot[...] = cot_in[...].astype(F32)
    lanes = lax.broadcasted_iota(jnp.int32, (48, 128), 1)
    acc = jnp.zeros((48, 128), F32)
    for row in range(count):
        u, v, t, k, g, wet2 = masked_row(ocean, kappa, depth, cot, row, scale)
        line = jnp.concatenate([u, v, t, k, g], axis=0)
        for f, field in enumerate((u, v, t, k)):
            f_a[row + WIDE, f] = field
        g_own[row + 1, 0] = g.astype(BF16).astype(F32)
        wet2s[row] = wet2
        rows[row] = line.astype(BF16)
        acc = jnp.where(lanes // 8 == row, pltpu.roll(line, (4 + 8 * row) % 128, axis=1), acc)
    packed[...] = acc.astype(BF16)

    sides_open = has_north.astype(jnp.int32) + has_south.astype(jnp.int32)
    pl.semaphore_wait(barrier, n_lon + n_lat - 2 + 2 * sides_open)

    def send_rows(start, dst, slot, to_lat):
        return pltpu.make_async_remote_copy(
            src_ref=rows.at[pl.ds(start, WIDE), pl.ds(0, 32)], dst_ref=dst, send_sem=row_send.at[slot],
            recv_sem=row_recv.at[slot], device_id=(lon, to_lat), device_id_type=MESH,
        )

    def send_g(start, dst, slot, to_lat):
        return pltpu.make_async_remote_copy(
            src_ref=rows.at[start, pl.ds(32, 16)], dst_ref=dst, send_sem=g_send.at[slot],
            recv_sem=g_recv.at[slot], device_id=(lon, to_lat), device_id_type=MESH,
        )

    def send_side(slot, to_lat, to_lon):
        return pltpu.make_async_remote_copy(
            src_ref=packed, dst_ref=sides.at[slot], send_sem=side_send.at[slot],
            recv_sem=side_recv.at[slot], device_id=(to_lon, to_lat), device_id_type=MESH,
        )

    def send_top(step):
        return pltpu.make_async_remote_copy(
            src_ref=rows.at[pl.ds(count - 2, 2), pl.ds(0, 32)], dst_ref=tops.at[lon], send_sem=top_send.at[step],
            recv_sem=top_recv.at[lon], device_id=(lax.rem(lon + step, n_lon), lat), device_id_type=MESH,
        )

    def top_from(step):
        peer = lax.rem(lon + step, n_lon)
        return pltpu.make_async_remote_copy(
            src_ref=rows.at[pl.ds(count - 2, 2), pl.ds(0, 32)], dst_ref=tops.at[peer], send_sem=top_send.at[step],
            recv_sem=top_recv.at[peer], device_id=(peer, lat), device_id_type=MESH,
        )

    to_north = send_rows(count - WIDE, south, 0, lat + 1)
    to_south = send_rows(0, north, 1, lat - 1)
    g_north = send_g(count - 1, south_g, 0, lat + 1)
    g_south = send_g(0, north_g, 1, lat - 1)
    same = [send_side(0, lat, east), send_side(1, lat, west)]
    up = [send_side(2, lat + 1, east), send_side(3, lat + 1, west)]
    down = [send_side(4, lat - 1, east), send_side(5, lat - 1, west)]

    for copy in same:
        copy.start()

    @pl.when(at_top)
    def _():
        for step in range(1, n_lon):
            send_top(step).start()

    @pl.when(has_north)
    def _():
        to_north.start()

    @pl.when(has_south)
    def _():
        to_south.start()

    @pl.when(has_north)
    def _():
        for copy in up:
            copy.start()
        g_north.start()

    @pl.when(has_south)
    def _():
        for copy in down:
            copy.start()
        g_south.start()


    def placed(height, width, shift):
        at = lax.broadcasted_iota(jnp.int32, (height, width), 0)
        to = lax.broadcasted_iota(jnp.int32, (height, width), 1)
        return jnp.where(at + shift == to, 1.0, 0.0).astype(BF16)

    for load in loads[4:]:
        load.wait()
    first = lat * count - WIDE
    row_total = count * n_lat
    row_ids = first + lax.broadcasted_iota(jnp.int32, coriolis.shape, 0)
    mirrored = jnp.where(row_ids >= row_total, 2 * row_total - 1 - row_ids, row_ids)
    coriolis[...] = 0.25 * jnp.sin(math.pi * (mirrored.astype(F32) + 0.5) / row_total - 0.5 * math.pi)
    krow[...], klane[...] = entry_place(active[...])
    wide_w = dot_first(first_w[0], placed(24, 224, 0))
    for k in range(1, 9):
        wide_w += dot_first(first_w[k], placed(24, 224, 24 * k))
    w_first[...] = wide_w.astype(BF16)
    for k in range(3):
        w_last[k] = sum(dot(last_w[3 * k + i], placed(64, 192, 64 * i)) for i in range(3)).astype(BF16)
    back_w = jnp.concatenate([last_w[k].astype(F32) for k in range(9)], axis=0)
    w_back[...] = back_w.T.astype(BF16)
    w_mix_t[...] = mix_w[...].astype(F32).T.astype(BF16)
    at_row = lax.broadcasted_iota(jnp.int32, (256, 128), 0)
    at_lane = lax.broadcasted_iota(jnp.int32, (128, 128), 0)
    for j in range(krow.shape[0]):
        picks[:, 128 * j : 128 * j + 128] = jnp.where(at_row == krow[j : j + 1, :], 1.0, 0.0).astype(BF16)

    @pl.when(at_top)
    def _():
        nx = n_lon * 128
        s = fold[0:1, 0:1]
        at = lax.broadcasted_iota(jnp.int32, (128, 256), 0)
        pos = lax.broadcasted_iota(jnp.int32, (1, 256), 1)
        col = lon * 128 + jnp.where(pos >= 192, pos - 256, pos)
        col = jnp.where(col < 0, col + nx, col)
        col = jnp.where(col >= nx, col - nx, col)
        partner = s - col
        partner = jnp.where(partner < 0, partner + nx, partner)
        for j in range(n_lon):
            partner_pick[j] = jnp.where(at + 128 * j == partner, 1.0, 0.0).astype(BF16)

    total = count + 2 * WIDE
    at_bottom = lat == 0
    lane = lax.broadcasted_iota(jnp.int32, (8, 128), 1)
    level = lax.broadcasted_iota(jnp.int32, (8, 128), 0)
    lane48 = lax.broadcasted_iota(jnp.int32, (48, 128), 1)
    zero32 = jnp.zeros((32, 128), F32)
    zero48 = jnp.zeros((48, 128), F32)

    def merge(low):
        odd = lane48 % 8 >= 4
        return jnp.where(odd, sides[low + 1].astype(F32), sides[low].astype(F32))

    def put(row, own, rim):
        for f in range(4):
            if own is not None:
                f_a[row, f] = own[8 * f : 8 * f + 8]
            f_b[row, f] = rim[8 * f : 8 * f + 8]
        if WIDE - 1 <= row <= WIDE + count:
            g_own[row - WIDE + 1, 1] = rim[32:48]

    def unpack(side, row):
        return pltpu.roll(side, (128 - 4 - 8 * row) % 128, axis=1)

    def roots(r, _):
        k_a, k_b = f_a[r, 3], f_b[r, 3]
        e_a, e_b = east_of(k_a, k_b, lane)
        ks_a[r, 0] = jnp.sqrt(k_a * e_a)
        ks_b[r, 0] = jnp.sqrt(k_b * e_b)
        ks_a[r, 1] = jnp.sqrt(k_a * f_a[r + 1, 3])
        ks_b[r, 1] = jnp.sqrt(k_b * f_b[r + 1, 3])
        return 0

    def summed(x):
        for d in (1, 2, 4):
            x = x + jnp.where(level >= d, pltpu.roll(x, d, axis=0), 0.0)
        return x

    def step(src_a, src_b, dst_a, dst_b):
        def body(r, _):
            fr = coriolis[pl.ds(r, 1), :]
            ke_a, ke_b = ks_a[r, 0], ks_b[r, 0]
            kw_a, kw_b = west_of(ke_a, ke_b, lane)
            coef = ((ke_a, kw_a, ks_a[r, 1], ks_a[r - 1, 1]), (ke_b, kw_b, ks_b[r, 1], ks_b[r - 1, 1]))
            mids, es, ws = [], [], []
            for f in range(3):
                a, b = src_a[r, f], src_b[r, f]
                mids.append((a, b))
                es.append(east_of(a, b, lane))
                ws.append(west_of(a, b, lane))
            for i, (src, dst, k_own) in enumerate(((src_a, dst_a, f_a[r, 3]), (src_b, dst_b, f_b[r, 3]))):
                wet = jnp.where(k_own > 0, 1.0, 0.0)
                ke, kw, kn, ks = coef[i]
                u, v, t = mids[0][i], mids[1][i], mids[2][i]
                ns = [src[r + 1, f] for f in range(3)]
                ss = [src[r - 1, f] for f in range(3)]
                outs = []
                for f in range(3):
                    m = mids[f][i]
                    outs.append(
                        m + ke * (es[f][i] - m) + kw * (ws[f][i] - m) + kn * (ns[f] - m) + ks * (ss[f] - m)
                    )
                dx = es[2][i] - ws[2][i]
                dy = ns[2] - ss[2]
                dst[r, 0] = wet * (outs[0] + fr * v - 0.025 * summed(dx))
                dst[r, 1] = wet * (outs[1] - fr * u - 0.025 * summed(dy))
                dst[r, 2] = wet * (outs[2] - 0.125 * (u * dx + v * dy))
            return 0

        return body

    first_step = step(f_a, f_b, h_a, h_b)
    for copy in same:
        copy.wait()
    mid = merge(0)
    for row in range(count):
        put(row + WIDE, None, unpack(mid, row))
    low, high = WIDE, WIDE + count - 1
    lax.fori_loop(low, high, roots, 0, unroll=3)
    lax.fori_loop(low + 1, high, first_step, 0, unroll=2)

    @pl.when(has_north)
    def _():
        to_north.wait_send()
        to_south.wait_recv()
        g_north.wait_send()
        g_south.wait_recv()
        for copy in up:
            copy.wait_send()
        for copy in down:
            copy.wait_recv()

    @pl.when(has_south)
    def _():
        to_south.wait_send()
        to_north.wait_recv()
        g_south.wait_send()
        g_north.wait_recv()
        for copy in down:
            copy.wait_send()
        for copy in up:
            copy.wait_recv()

    @pl.when(at_top)
    def _():
        tops[lon] = rows[count - 2 : count, 0:32]
        for step in range(1, n_lon):
            send_top(step).wait_send()
            top_from(step).wait_recv()

    below = jnp.where(at_bottom, zero48, merge(2))
    above = jnp.where(at_top, zero48, merge(4))
    for row in range(WIDE):
        put(row, jnp.where(at_bottom, zero32, south[row].astype(F32)), unpack(below, count - WIDE + row))
        put(WIDE + count + row, jnp.where(at_top, zero32, north[row].astype(F32)), unpack(above, row))

    g_own[0, 0] = jnp.where(at_bottom, zero48[:16], south_g[...].astype(F32))
    g_own[count + 1, 0] = jnp.where(at_top, zero48[:16], north_g[...].astype(F32))

    @pl.when(at_top)
    def _():
        res = jnp.zeros((64, 256), F32)
        for j in range(n_lon):
            both = jnp.concatenate([tops[j, 1, 0:32], tops[j, 0, 0:32]], axis=0)
            res = res + dot(both, partner_pick[j])
        for q in range(2):
            for f in range(4):
                sign = -1.0 if f < 2 else 1.0
                part = sign * res[32 * q + 8 * f : 32 * q + 8 * f + 8]
                f_a[WIDE + count + q, f] = part[:, :128]
                f_b[WIDE + count + q, f] = part[:, 128:]

    lax.fori_loop(0, low, roots, 0, unroll=True)
    lax.fori_loop(high, total - 1, roots, 0, unroll=True)
    lax.fori_loop(1, low + 1, first_step, 0, unroll=2)
    lax.fori_loop(high, total - 1, first_step, 0, unroll=2)
    lax.fori_loop(2, total - 2, step(h_a, h_b, f_a, f_b), 0, unroll=2)

    lane24 = lax.broadcasted_iota(jnp.int32, (24, 128), 1)
    lane72 = lax.broadcasted_iota(jnp.int32, (72, 128), 1)
    pad8 = jnp.zeros((8, 128), F32)
    lines = []
    side = jnp.zeros((72, 128), F32)
    for q in range(count + 4):
        a = jnp.concatenate([f_a[q + 2, f] for f in range(3)], axis=0)
        b = jnp.concatenate([f_b[q + 2, f] for f in range(3)], axis=0)
        if q < 2:
            a, b = jnp.where(at_bottom, 0.0, a), jnp.where(at_bottom, 0.0, b)
        if q >= count + 2:
            a, b = jnp.where(at_top, 0.0, a), jnp.where(at_top, 0.0, b)
        e_a, e_b = east_of(a, b, lane24)
        w_a, w_b = west_of(a, b, lane24)
        lines.append(jnp.concatenate([w_a, a, e_a], axis=0))
        rim = jnp.concatenate([w_b, b, e_b], axis=0)
        side = jnp.where(lane72 // 2 == q, pltpu.roll(rim, (1 + 2 * q) % 128, axis=1), side)
        if q >= 2:
            r = q - 2
            patches[:, 128 * r : 128 * r + 128] = jnp.concatenate(lines[-3:] + [pad8], axis=0).astype(BF16)
    span = (count + 2) * 128
    patches[:, span : span + 128] = jnp.concatenate(
        [side, pltpu.roll(side, 126, axis=1), pltpu.roll(side, 124, axis=1), pad8], axis=0
    ).astype(BF16)
    patches[:, span + 128 :] = jnp.zeros((224, patches.shape[1] - span - 128), BF16)

    for start in range(0, patches.shape[1], 256):
        pre1 = dot(w_first[...], patches[:, start : start + 256])
        s1 = sigmoid(pre1)
        h1 = (pre1 * s1).astype(BF16)
        pre2 = dot(mix_w[...], h1)
        s2 = sigmoid(pre2)
        hid1[:, start : start + 256] = h1
        hid2[:, start : start + 256] = (pre2 * s2).astype(BF16).astype(F32)
        slope1[:, start : start + 256] = slope(pre1, s1)
        slope2[:, start : start + 256] = slope(pre2, s2)

    lane64 = lax.broadcasted_iota(jnp.int32, (64, 128), 1)
    lane16 = lax.broadcasted_iota(jnp.int32, (16, 128), 1)
    edge = hid2[:, span : span + 128]
    for r in range(count + 2):
        own = hid2[:, 128 * r : 128 * r + 128]
        to_w = jnp.where(lane64 == 0, pltpu.roll(edge, (128 - 2 * r) % 128, axis=1), pltpu.roll(own, 1, axis=1))
        to_e = jnp.where(lane64 == 127, pltpu.roll(edge, 126 - 2 * r, axis=1), pltpu.roll(own, 127, axis=1))
        both = jnp.concatenate([to_w, own, to_e], axis=0)
        if r == 0:
            both = jnp.where(at_bottom, 0.0, both)
        if r == count + 1:
            both = jnp.where(at_top, 0.0, both)
        hshift[:, 128 * r : 128 * r + 128] = both.astype(BF16)
    glines = []
    for r in range(count + 2):
        a, b = g_own[r, 0], g_own[r, 1]
        e_a, _ = east_of(a, b, lane16)
        w_a, _ = west_of(a, b, lane16)
        glines.append(jnp.concatenate([e_a, a, w_a], axis=0))
        if r >= 2:
            j = r - 2
            gpatch[:, 128 * j : 128 * j + 128] = jnp.concatenate(glines[-3:][::-1], axis=0).astype(BF16)

    cells = count * 128
    for start in range(0, cells, 256):
        here = slice(start, start + 256)
        near = slice(start + 128, start + 384)
        back = dot(w_back[...], gpatch[:, here])
        dm = (back * slope2[:, near]).astype(BF16)
        dmix[:, here] = dm
        dfirst[:, here] = (dot(w_mix_t[...], dm) * slope1[:, near]).astype(BF16)

    g_first = dot_cells(dfirst[...], patches[:, 128 : 128 + cells])
    g_mix = dot_cells(dmix[...], hid1[:, 128 : 128 + cells])
    g_mid = gpatch[64:80, :]
    g_last = jnp.concatenate([dot_cells(g_mid, hshift[:, 128 * i : 128 * i + cells]) for i in range(3)], axis=1)
    table[0:64, :] = g_first[:, :128]
    table[64:128, 0:96] = g_first[:, 128:224]
    table[64:128, 96:128] = jnp.zeros((64, 32), F32)
    table[128:192, 64:128] = jnp.zeros((64, 64), F32)
    table[128:192, 0:64] = g_mix
    table[128:144, 64:128] = g_last[:, 512:576]
    for i in range(4):
        table[192 + 16 * i : 208 + 16 * i, :] = g_last[:, 128 * i : 128 * i + 128]
    q = table[...].T
    hi = q.astype(BF16)
    lo = (q - hi.astype(F32)).astype(BF16)
    split = jnp.concatenate([hi, lo], axis=0)
    per = picked.shape[1]
    for j in range(0, krow.shape[0], 2):
        got = dot(split, picks[:, 128 * j : 128 * j + 256])
        got = got[:128] + got[128:]
        for i in range(2):
            mine = jnp.where(at_lane == klane[j + i : j + i + 1, :], got[:, 128 * i : 128 * i + 128], 0.0)
            to = (j + i) // per
            picked[to, (j + i) % per : (j + i) % per + 1, :] = jnp.sum(mine, axis=0, keepdims=True)

    lons = [lax.rem(lon + step, n_lon) for step in range(1, n_lon)]
    lats = [lax.rem(lat + step, n_lat) for step in range(1, n_lat)]
    def share(src, dst, ssem, rsem, to):
        return pltpu.make_async_remote_copy(
            src_ref=src, dst_ref=dst, send_sem=ssem, recv_sem=rsem, device_id=to, device_id_type=MESH
        )

    first = [share(picked.at[to], got_lon.at[lon], out_sem1.at[to], in_sem1.at[lon], (to, lat)) for to in lons]
    for c in first:
        c.start()
    got_lon[lon] = picked[lon]

    for start in range(0, cells, 256):
        tend = dot(w_last[0], hshift[:, start : start + 256])
        tend += dot(w_last[1], hshift[:, start + 128 : start + 384])
        tend += dot(w_last[2], hshift[:, start + 256 : start + 512])
        for j in range(2):
            r = start // 128 + j
            closing[:, r, :] = wet2s[r] * tend[:, 128 * j : 128 * j + 128]
    closure_out[...] = closing[...].astype(BF16)
    save_closure = pltpu.make_async_copy(closure_out, closure, out_sem.at[0])
    save_closure.start()
    for row in range(count):
        for f in range(3):
            state_out[f, :, row, :] = f_a[row + WIDE, f]
    save_state = pltpu.make_async_copy(state_out, state, out_sem.at[1])
    save_state.start()
    for c, to in zip(first, lons):
        c.wait_send()
        share(picked.at[to], got_lon.at[to], out_sem1.at[to], in_sem1.at[to], (to, lat)).wait_recv()
    got_lat[lat] = jnp.sum(got_lon[...], axis=0)
    second = [share(got_lat.at[lat], got_lat.at[lat], out_sem2.at[to], in_sem2.at[lat], (lon, to)) for to in lats]
    for c in second:
        c.start()
    for c, to in zip(second, lats):
        c.wait_send()
        share(got_lat.at[to], got_lat.at[to], out_sem2.at[to], in_sem2.at[to], (lon, to)).wait_recv()
    chunk[...] = jnp.sum(got_lat[...], axis=0)
    third = [share(chunk, out.at[lon], out_sem3.at[to], in_sem3.at[lon], (to, lat)) for to in lons]
    for c in third:
        c.start()
    save_chunk = pltpu.make_async_copy(chunk, out.at[lon], out_sem.at[2])
    save_chunk.start()
    for c, to in zip(third, lons):
        c.wait_send()
        share(chunk, out.at[to], out_sem3.at[to], in_sem3.at[to], (to, lat)).wait_recv()
    for save in (save_chunk, save_state, save_closure):
        save.wait()


def entry_place(index):
    def parts(value, size):
        whole = jnp.floor((value.astype(F32) + 0.5) * (1.0 / size)).astype(jnp.int32)
        return whole, value - size * whole

    k, rest = parts(index, 1536)
    o, c = parts(rest, 24)
    col = k * 24 + c
    row_f, lane_f = o + 64 * (col >> 7), col & 127
    m = index - 13824
    row_m, lane_m = 128 + (m >> 6), m & 63
    m = index - 17920
    o, col = (m & 1023) >> 6, (m >> 10) * 64 + (m & 63)
    spill = col >= 512
    row_l = jnp.where(spill, 128 + o, 192 + 16 * (col >> 7) + o)
    lane_l = jnp.where(spill, 64 + col - 512, col & 127)
    row = jnp.where(index < 13824, row_f, jnp.where(index < 17920, row_m, row_l))
    lane = jnp.where(index < 13824, lane_f, jnp.where(index < 17920, lane_m, lane_l))
    return row, lane


def on_device(
    n_lon, n_lat, ocean_state, diffusivity, depth_levels, fold_pair, first_weight, mix_weight, last_weight,
    cotangent, active_index,
):
    count = ocean_state.shape[2]
    row_total = count * n_lat
    scale = 1.0 / math.sqrt(row_total * 128 * n_lon)
    sds = jax.ShapeDtypeStruct
    dma = pltpu.SemaphoreType.DMA
    vmem = pltpu.VMEM
    picks = active_index.shape[0] // 128
    depth = picks // n_lon
    total = count + 2 * WIDE
    wide = (count + 4) * 128
    cells = count * 128
    operands = (
        ocean_state, diffusivity, depth_levels, cotangent, fold_pair.reshape(-1, 128),
        jnp.transpose(first_weight, (0, 2, 1)), mix_weight, last_weight, active_index.reshape(picks, 128),
    )
    outs = [
        sds((3, 8, count, 128), F32), sds((16, count, 128), BF16), sds((n_lon, depth, 128), F32),
    ]
    state, closure, reduced = pl.pallas_call(
        functools.partial(kernel, n_lon, n_lat, scale),
        out_shape=outs,
        in_specs=[HBM] * 9,
        out_specs=[ANY] * 3,
        scratch_shapes=[vmem(x.shape, x.dtype) for x in operands] + [
            dma((9,)), vmem((picks, 128), jnp.int32), vmem((picks, 128), jnp.int32), vmem((total, 128), F32),
            vmem((16, 128), BF16), vmem((16, 128), BF16),
            vmem((16, count, 128), F32), vmem((16, count, 128), F32),
            vmem((WIDE, 32, 128), BF16), vmem((WIDE, 32, 128), BF16), vmem((6, 48, 128), BF16),
            vmem((n_lon, 2, 32, 128), BF16), vmem((count, 48, 128), BF16), vmem((48, 128), BF16),
            vmem((n_lon, 128, 256), BF16), vmem((256, picks * 128), BF16),
            vmem((64, 224), BF16), vmem((3, 16, 192), BF16), vmem((64, 144), BF16), vmem((64, 64), BF16),
            vmem((total, 4, 8, 128), F32), vmem((total, 4, 8, 128), F32),
            vmem((total, 3, 8, 128), F32), vmem((total, 3, 8, 128), F32),
            vmem((total, 2, 8, 128), F32), vmem((total, 2, 8, 128), F32),
            vmem((count + 2, 2, 16, 128), F32), vmem((count, 16, 128), F32),
            vmem((224, wide), BF16), vmem((64, wide), F32), vmem((64, wide), F32),
            vmem((64, wide), BF16), vmem((64, wide), F32), vmem((192, (count + 2) * 128), BF16),
            vmem((144, cells), BF16), vmem((64, cells), BF16), vmem((64, cells), BF16),
            vmem((256, 128), F32),
            vmem((n_lon, depth, 128), F32), vmem((n_lon, depth, 128), F32), vmem((n_lat, depth, 128), F32),
            vmem((depth, 128), F32), vmem((3, 8, count, 128), F32), vmem((16, count, 128), BF16), dma((3,)),
            dma((2,)), dma((2,)), dma((2,)), dma((2,)), dma((6,)), dma((6,)), dma((n_lon,)), dma((n_lon,)),
            dma((n_lon,)), dma((n_lon,)), dma((n_lat,)), dma((n_lat,)), dma((n_lon,)), dma((n_lon,)),
        ],
        compiler_params=pltpu.CompilerParams(
            collective_id=0, has_side_effects=True, vmem_limit_bytes=GRANT
        ),
        name="ocean",
    )(*operands)
    return state, closure, reduced.reshape(-1)


def solution(mesh):
    in_specs = (
        P(None, None, "lat", "lon"), P(None, "lat", "lon"), P("lat", "lon"), P(), P(), P(), P(),
        P(None, "lat", "lon"), P(),
    )
    out_specs = (P(None, None, "lat", "lon"), P(None, "lat", "lon"), P())
    return jax.shard_map(
        functools.partial(on_device, mesh.shape["lon"], mesh.shape["lat"]),
        mesh=mesh, in_specs=in_specs, out_specs=out_specs, check_vma=False,
    )
```

```python
import functools
import math

import jax
import jax.numpy as jnp
from jax import lax
from jax.experimental import pallas as pl
from jax.experimental.pallas import tpu as pltpu
from jax.sharding import PartitionSpec as P

MESH = pl.DeviceIdType.MESH
F32 = jnp.float32
BF16 = jnp.bfloat16
GRANT = 62 * 1024 * 1024
WIDE = 4
HBM = pl.BlockSpec(memory_space=pltpu.HBM)
ANY = pl.BlockSpec(memory_space=pl.ANY)


def masked_row(ocean, kappa, depth, cot, row, scale):
    levels = lax.broadcasted_iota(jnp.int32, (8, 128), 0)
    wet = (levels < depth[pl.ds(row, 1), :]).astype(F32)
    u = ocean[0, :, row, :] * wet
    v = ocean[1, :, row, :] * wet
    t = ocean[2, :, row, :] * wet
    k = kappa[:, row, :] * wet
    wet2 = jnp.concatenate([wet, wet], axis=0)
    g = scale * wet2 * cot[:, row, :]
    return u, v, t, k, g, wet2


def dot(a, b):
    return jnp.dot(a, b, preferred_element_type=F32)


def dot_cells(a, b):
    return lax.dot_general(a, b, (((1,), (1,)), ((), ())), preferred_element_type=F32)


def dot_first(a, b):
    return lax.dot_general(a, b, (((0,), (0,)), ((), ())), preferred_element_type=F32)


def slope(pre, sigma):
    return sigma * (1.0 + pre * (1.0 - sigma))


def sigmoid(pre):
    return 0.5 + 0.5 * jnp.tanh(0.5 * pre)


def east_of(own, rim, lane):
    a = pltpu.roll(own, 127, axis=own.ndim - 1)
    b = pltpu.roll(rim, 127, axis=own.ndim - 1)
    return jnp.where(lane == 127, b, a), jnp.where(lane == 127, a, b)


def west_of(own, rim, lane):
    a = pltpu.roll(own, 1, axis=own.ndim - 1)
    b = pltpu.roll(rim, 1, axis=own.ndim - 1)
    return jnp.where(lane == 0, b, a), jnp.where(lane == 0, a, b)


def kernel(
    n_lon, n_lat, scale, *refs,
):
    operands, refs = refs[:9], refs[9:]
    outputs, refs = refs[:3], refs[3:]
    held, refs = refs[:9], refs[9:]
    loads = [pltpu.make_async_copy(a, b, refs[0].at[i]) for i, (a, b) in enumerate(zip(operands, held))]
    for i in (0, 1, 2, 3, 5, 6, 7, 8, 4):
        loads[i].start()
    ocean_step(n_lon, n_lat, scale, loads, *held, *outputs, *refs[1:])


def ocean_step(
    n_lon, n_lat, scale, loads, ocean, kappa, depth, cot_in, fold, first_w, mix_w, last_w, active,
    state, closure, out,
    krow, klane, coriolis, north_g, south_g, cot, closing, north, south, sides, tops, rows, packed, partner_pick, picks, w_first, w_last, w_back, w_mix_t,
    f_a, f_b, h_a, h_b, ks_a, ks_b, g_own, wet2s, patches, slope1, slope2, hid1, hid2, hshift, gpatch, dmix, dfirst, table,
    picked, got_lon, got_lat, chunk, state_out, closure_out, out_sem,
    row_send, row_recv, g_send, g_recv, side_send, side_recv, top_send, top_recv, out_sem1, in_sem1, out_sem2, in_sem2, out_sem3, in_sem3,
):
    lon = lax.axis_index("lon")
    lat = lax.axis_index("lat")
    count = rows.shape[0]
    east = lax.rem(lon + 1, n_lon)
    west = lax.rem(lon + n_lon - 1, n_lon)
    has_north = lat < n_lat - 1
    has_south = lat > 0
    at_top = lat == n_lat - 1

    barrier = pltpu.get_barrier_semaphore()

    def greet(to_lat, to_lon):
        pl.semaphore_signal(barrier, inc=1, device_id=(to_lon, to_lat), device_id_type=MESH)

    for step in range(1, n_lon):
        greet(lat, lax.rem(lon + step, n_lon))
    for step in range(1, n_lat):
        greet(lax.rem(lat + step, n_lat), lon)

    @pl.when(has_north)
    def _():
        for to in (east, west):
            greet(lat + 1, to)

    @pl.when(has_south)
    def _():
        for to in (east, west):
            greet(lat - 1, to)

    for load in loads[:4]:
        load.wait()
    cot[...] = cot_in[...].astype(F32)
    lanes = lax.broadcasted_iota(jnp.int32, (48, 128), 1)
    acc = jnp.zeros((48, 128), F32)
    for row in range(count):
        u, v, t, k, g, wet2 = masked_row(ocean, kappa, depth, cot, row, scale)
        line = jnp.concatenate([u, v, t, k, g], axis=0)
        for f, field in enumerate((u, v, t, k)):
            f_a[row + WIDE, f] = field
        g_own[row + 1, 0] = g.astype(BF16).astype(F32)
        wet2s[row] = wet2
        rows[row] = line.astype(BF16)
        acc = jnp.where(lanes // 8 == row, pltpu.roll(line, (4 + 8 * row) % 128, axis=1), acc)
    packed[...] = acc.astype(BF16)

    sides_open = has_north.astype(jnp.int32) + has_south.astype(jnp.int32)
    pl.semaphore_wait(barrier, n_lon + n_lat - 2 + 2 * sides_open)

    def send_rows(start, dst, slot, to_lat):
        return pltpu.make_async_remote_copy(
            src_ref=rows.at[pl.ds(start, WIDE), pl.ds(0, 32)], dst_ref=dst, send_sem=row_send.at[slot],
            recv_sem=row_recv.at[slot], device_id=(lon, to_lat), device_id_type=MESH,
        )

    def send_g(start, dst, slot, to_lat):
        return pltpu.make_async_remote_copy(
            src_ref=rows.at[start, pl.ds(32, 16)], dst_ref=dst, send_sem=g_send.at[slot],
            recv_sem=g_recv.at[slot], device_id=(lon, to_lat), device_id_type=MESH,
        )

    def send_side(slot, to_lat, to_lon):
        return pltpu.make_async_remote_copy(
            src_ref=packed, dst_ref=sides.at[slot], send_sem=side_send.at[slot],
            recv_sem=side_recv.at[slot], device_id=(to_lon, to_lat), device_id_type=MESH,
        )

    def send_top(step):
        return pltpu.make_async_remote_copy(
            src_ref=rows.at[pl.ds(count - 2, 2), pl.ds(0, 32)], dst_ref=tops.at[lon], send_sem=top_send.at[step],
            recv_sem=top_recv.at[lon], device_id=(lax.rem(lon + step, n_lon), lat), device_id_type=MESH,
        )

    def top_from(step):
        peer = lax.rem(lon + step, n_lon)
        return pltpu.make_async_remote_copy(
            src_ref=rows.at[pl.ds(count - 2, 2), pl.ds(0, 32)], dst_ref=tops.at[peer], send_sem=top_send.at[step],
            recv_sem=top_recv.at[peer], device_id=(peer, lat), device_id_type=MESH,
        )

    to_north = send_rows(count - WIDE, south, 0, lat + 1)
    to_south = send_rows(0, north, 1, lat - 1)
    g_north = send_g(count - 1, south_g, 0, lat + 1)
    g_south = send_g(0, north_g, 1, lat - 1)
    same = [send_side(0, lat, east), send_side(1, lat, west)]
    up = [send_side(2, lat + 1, east), send_side(3, lat + 1, west)]
    down = [send_side(4, lat - 1, east), send_side(5, lat - 1, west)]

    for copy in same:
        copy.start()

    @pl.when(at_top)
    def _():
        for step in range(1, n_lon):
            send_top(step).start()

    @pl.when(has_north)
    def _():
        to_north.start()

    @pl.when(has_south)
    def _():
        to_south.start()

    @pl.when(has_north)
    def _():
        for copy in up:
            copy.start()
        g_north.start()

    @pl.when(has_south)
    def _():
        for copy in down:
            copy.start()
        g_south.start()


    def placed(height, width, shift):
        at = lax.broadcasted_iota(jnp.int32, (height, width), 0)
        to = lax.broadcasted_iota(jnp.int32, (height, width), 1)
        return jnp.where(at + shift == to, 1.0, 0.0).astype(BF16)

    for load in loads[4:]:
        load.wait()
    first = lat * count - WIDE
    row_total = count * n_lat
    row_ids = first + lax.broadcasted_iota(jnp.int32, coriolis.shape, 0)
    mirrored = jnp.where(row_ids >= row_total, 2 * row_total - 1 - row_ids, row_ids)
    coriolis[...] = 0.25 * jnp.sin(math.pi * (mirrored.astype(F32) + 0.5) / row_total - 0.5 * math.pi)
    krow[...], klane[...] = entry_place(active[...])
    wide_w = dot_first(first_w[0], placed(24, 224, 0))
    for k in range(1, 9):
        wide_w += dot_first(first_w[k], placed(24, 224, 24 * k))
    w_first[...] = wide_w.astype(BF16)
    for k in range(3):
        w_last[k] = sum(dot(last_w[3 * k + i], placed(64, 192, 64 * i)) for i in range(3)).astype(BF16)
    back_w = jnp.concatenate([last_w[k].astype(F32) for k in range(9)], axis=0)
    w_back[...] = back_w.T.astype(BF16)
    w_mix_t[...] = mix_w[...].astype(F32).T.astype(BF16)
    at_row = lax.broadcasted_iota(jnp.int32, (256, 128), 0)
    at_lane = lax.broadcasted_iota(jnp.int32, (128, 128), 0)
    for j in range(krow.shape[0]):
        picks[:, 128 * j : 128 * j + 128] = jnp.where(at_row == krow[j : j + 1, :], 1.0, 0.0).astype(BF16)

    @pl.when(at_top)
    def _():
        nx = n_lon * 128
        s = fold[0:1, 0:1]
        at = lax.broadcasted_iota(jnp.int32, (128, 256), 0)
        pos = lax.broadcasted_iota(jnp.int32, (1, 256), 1)
        col = lon * 128 + jnp.where(pos >= 192, pos - 256, pos)
        col = jnp.where(col < 0, col + nx, col)
        col = jnp.where(col >= nx, col - nx, col)
        partner = s - col
        partner = jnp.where(partner < 0, partner + nx, partner)
        for j in range(n_lon):
            partner_pick[j] = jnp.where(at + 128 * j == partner, 1.0, 0.0).astype(BF16)

    total = count + 2 * WIDE
    at_bottom = lat == 0
    lane = lax.broadcasted_iota(jnp.int32, (8, 128), 1)
    level = lax.broadcasted_iota(jnp.int32, (8, 128), 0)
    lane48 = lax.broadcasted_iota(jnp.int32, (48, 128), 1)
    zero32 = jnp.zeros((32, 128), F32)
    zero48 = jnp.zeros((48, 128), F32)

    def merge(low):
        odd = lane48 % 8 >= 4
        return jnp.where(odd, sides[low + 1].astype(F32), sides[low].astype(F32))

    def put(row, own, rim):
        for f in range(4):
            if own is not None:
                f_a[row, f] = own[8 * f : 8 * f + 8]
            f_b[row, f] = rim[8 * f : 8 * f + 8]
        if WIDE - 1 <= row <= WIDE + count:
            g_own[row - WIDE + 1, 1] = rim[32:48]

    def unpack(side, row):
        return pltpu.roll(side, (128 - 4 - 8 * row) % 128, axis=1)

    def roots(r, _):
        k_a, k_b = f_a[r, 3], f_b[r, 3]
        e_a, e_b = east_of(k_a, k_b, lane)
        ks_a[r, 0] = jnp.sqrt(k_a * e_a)
        ks_b[r, 0] = jnp.sqrt(k_b * e_b)
        ks_a[r, 1] = jnp.sqrt(k_a * f_a[r + 1, 3])
        ks_b[r, 1] = jnp.sqrt(k_b * f_b[r + 1, 3])
        return 0

    def summed(x):
        for d in (1, 2, 4):
            x = x + jnp.where(level >= d, pltpu.roll(x, d, axis=0), 0.0)
        return x

    def step(src_a, src_b, dst_a, dst_b):
        def body(r, _):
            fr = coriolis[pl.ds(r, 1), :]
            ke_a, ke_b = ks_a[r, 0], ks_b[r, 0]
            kw_a, kw_b = west_of(ke_a, ke_b, lane)
            coef = ((ke_a, kw_a, ks_a[r, 1], ks_a[r - 1, 1]), (ke_b, kw_b, ks_b[r, 1], ks_b[r - 1, 1]))
            mids, es, ws = [], [], []
            for f in range(3):
                a, b = src_a[r, f], src_b[r, f]
                mids.append((a, b))
                es.append(east_of(a, b, lane))
                ws.append(west_of(a, b, lane))
            for i, (src, dst, k_own) in enumerate(((src_a, dst_a, f_a[r, 3]), (src_b, dst_b, f_b[r, 3]))):
                wet = jnp.where(k_own > 0, 1.0, 0.0)
                ke, kw, kn, ks = coef[i]
                u, v, t = mids[0][i], mids[1][i], mids[2][i]
                ns = [src[r + 1, f] for f in range(3)]
                ss = [src[r - 1, f] for f in range(3)]
                outs = []
                for f in range(3):
                    m = mids[f][i]
                    outs.append(
                        m + ke * (es[f][i] - m) + kw * (ws[f][i] - m) + kn * (ns[f] - m) + ks * (ss[f] - m)
                    )
                dx = es[2][i] - ws[2][i]
                dy = ns[2] - ss[2]
                dst[r, 0] = wet * (outs[0] + fr * v - 0.025 * summed(dx))
                dst[r, 1] = wet * (outs[1] - fr * u - 0.025 * summed(dy))
                dst[r, 2] = wet * (outs[2] - 0.125 * (u * dx + v * dy))
            return 0

        return body

    first_step = step(f_a, f_b, h_a, h_b)
    for copy in same:
        copy.wait()
    mid = merge(0)
    for row in range(count):
        put(row + WIDE, None, unpack(mid, row))
    low, high = WIDE, WIDE + count - 1
    lax.fori_loop(low, high, roots, 0, unroll=5)
    lax.fori_loop(low + 1, high, first_step, 0, unroll=7)

    @pl.when(has_north)
    def _():
        to_north.wait_send()
        to_south.wait_recv()
        g_north.wait_send()
        g_south.wait_recv()
        for copy in up:
            copy.wait_send()
        for copy in down:
            copy.wait_recv()

    @pl.when(has_south)
    def _():
        to_south.wait_send()
        to_north.wait_recv()
        g_south.wait_send()
        g_north.wait_recv()
        for copy in down:
            copy.wait_send()
        for copy in up:
            copy.wait_recv()

    @pl.when(at_top)
    def _():
        tops[lon] = rows[count - 2 : count, 0:32]
        for step in range(1, n_lon):
            send_top(step).wait_send()
            top_from(step).wait_recv()

    below = jnp.where(at_bottom, zero48, merge(2))
    above = jnp.where(at_top, zero48, merge(4))
    for row in range(WIDE):
        put(row, jnp.where(at_bottom, zero32, south[row].astype(F32)), unpack(below, count - WIDE + row))
        put(WIDE + count + row, jnp.where(at_top, zero32, north[row].astype(F32)), unpack(above, row))

    g_own[0, 0] = jnp.where(at_bottom, zero48[:16], south_g[...].astype(F32))
    g_own[count + 1, 0] = jnp.where(at_top, zero48[:16], north_g[...].astype(F32))

    @pl.when(at_top)
    def _():
        res = jnp.zeros((64, 256), F32)
        for j in range(n_lon):
            both = jnp.concatenate([tops[j, 1, 0:32], tops[j, 0, 0:32]], axis=0)
            res = res + dot(both, partner_pick[j])
        for q in range(2):
            for f in range(4):
                sign = -1.0 if f < 2 else 1.0
                part = sign * res[32 * q + 8 * f : 32 * q + 8 * f + 8]
                f_a[WIDE + count + q, f] = part[:, :128]
                f_b[WIDE + count + q, f] = part[:, 128:]

    lax.fori_loop(0, low, roots, 0, unroll=True)
    lax.fori_loop(high, total - 1, roots, 0, unroll=True)
    lax.fori_loop(1, low + 1, first_step, 0, unroll=True)
    lax.fori_loop(high, total - 1, first_step, 0, unroll=True)
    lax.fori_loop(2, total - 2, step(h_a, h_b, f_a, f_b), 0, unroll=5)

    lane24 = lax.broadcasted_iota(jnp.int32, (24, 128), 1)
    lane72 = lax.broadcasted_iota(jnp.int32, (72, 128), 1)
    pad8 = jnp.zeros((8, 128), F32)
    lines = []
    side = jnp.zeros((72, 128), F32)
    for q in range(count + 4):
        a = jnp.concatenate([f_a[q + 2, f] for f in range(3)], axis=0)
        b = jnp.concatenate([f_b[q + 2, f] for f in range(3)], axis=0)
        if q < 2:
            a, b = jnp.where(at_bottom, 0.0, a), jnp.where(at_bottom, 0.0, b)
        if q >= count + 2:
            a, b = jnp.where(at_top, 0.0, a), jnp.where(at_top, 0.0, b)
        e_a, e_b = east_of(a, b, lane24)
        w_a, w_b = west_of(a, b, lane24)
        lines.append(jnp.concatenate([w_a, a, e_a], axis=0))
        rim = jnp.concatenate([w_b, b, e_b], axis=0)
        side = jnp.where(lane72 // 2 == q, pltpu.roll(rim, (1 + 2 * q) % 128, axis=1), side)
        if q >= 2:
            r = q - 2
            patches[:, 128 * r : 128 * r + 128] = jnp.concatenate(lines[-3:] + [pad8], axis=0).astype(BF16)
    span = (count + 2) * 128
    patches[:, span : span + 128] = jnp.concatenate(
        [side, pltpu.roll(side, 126, axis=1), pltpu.roll(side, 124, axis=1), pad8], axis=0
    ).astype(BF16)
    patches[:, span + 128 :] = jnp.zeros((224, patches.shape[1] - span - 128), BF16)

    for start in range(0, patches.shape[1], 256):
        pre1 = dot(w_first[...], patches[:, start : start + 256])
        s1 = sigmoid(pre1)
        h1 = (pre1 * s1).astype(BF16)
        pre2 = dot(mix_w[...], h1)
        s2 = sigmoid(pre2)
        hid1[:, start : start + 256] = h1
        hid2[:, start : start + 256] = (pre2 * s2).astype(BF16).astype(F32)
        slope1[:, start : start + 256] = slope(pre1, s1)
        slope2[:, start : start + 256] = slope(pre2, s2)

    lane64 = lax.broadcasted_iota(jnp.int32, (64, 128), 1)
    lane16 = lax.broadcasted_iota(jnp.int32, (16, 128), 1)
    edge = hid2[:, span : span + 128]
    for r in range(count + 2):
        own = hid2[:, 128 * r : 128 * r + 128]
        to_w = jnp.where(lane64 == 0, pltpu.roll(edge, (128 - 2 * r) % 128, axis=1), pltpu.roll(own, 1, axis=1))
        to_e = jnp.where(lane64 == 127, pltpu.roll(edge, 126 - 2 * r, axis=1), pltpu.roll(own, 127, axis=1))
        both = jnp.concatenate([to_w, own, to_e], axis=0)
        if r == 0:
            both = jnp.where(at_bottom, 0.0, both)
        if r == count + 1:
            both = jnp.where(at_top, 0.0, both)
        hshift[:, 128 * r : 128 * r + 128] = both.astype(BF16)
    glines = []
    for r in range(count + 2):
        a, b = g_own[r, 0], g_own[r, 1]
        e_a, _ = east_of(a, b, lane16)
        w_a, _ = west_of(a, b, lane16)
        glines.append(jnp.concatenate([e_a, a, w_a], axis=0))
        if r >= 2:
            j = r - 2
            gpatch[:, 128 * j : 128 * j + 128] = jnp.concatenate(glines[-3:][::-1], axis=0).astype(BF16)

    cells = count * 128
    for start in range(0, cells, 256):
        here = slice(start, start + 256)
        near = slice(start + 128, start + 384)
        back = dot(w_back[...], gpatch[:, here])
        dm = (back * slope2[:, near]).astype(BF16)
        dmix[:, here] = dm
        dfirst[:, here] = (dot(w_mix_t[...], dm) * slope1[:, near]).astype(BF16)

    g_first = dot_cells(dfirst[...], patches[:, 128 : 128 + cells])
    g_mix = dot_cells(dmix[...], hid1[:, 128 : 128 + cells])
    g_mid = gpatch[64:80, :]
    g_last = jnp.concatenate([dot_cells(g_mid, hshift[:, 128 * i : 128 * i + cells]) for i in range(3)], axis=1)
    table[0:64, :] = g_first[:, :128]
    table[64:128, 0:96] = g_first[:, 128:224]
    table[64:128, 96:128] = jnp.zeros((64, 32), F32)
    table[128:192, 64:128] = jnp.zeros((64, 64), F32)
    table[128:192, 0:64] = g_mix
    table[128:144, 64:128] = g_last[:, 512:576]
    for i in range(4):
        table[192 + 16 * i : 208 + 16 * i, :] = g_last[:, 128 * i : 128 * i + 128]
    q = table[...].T
    hi = q.astype(BF16)
    lo = (q - hi.astype(F32)).astype(BF16)
    split = jnp.concatenate([hi, lo], axis=0)
    per = picked.shape[1]
    for j in range(0, krow.shape[0], 2):
        got = dot(split, picks[:, 128 * j : 128 * j + 256])
        got = got[:128] + got[128:]
        for i in range(2):
            mine = jnp.where(at_lane == klane[j + i : j + i + 1, :], got[:, 128 * i : 128 * i + 128], 0.0)
            to = (j + i) // per
            picked[to, (j + i) % per : (j + i) % per + 1, :] = jnp.sum(mine, axis=0, keepdims=True)

    lons = [lax.rem(lon + step, n_lon) for step in range(1, n_lon)]
    lats = [lax.rem(lat + step, n_lat) for step in range(1, n_lat)]
    def share(src, dst, ssem, rsem, to):
        return pltpu.make_async_remote_copy(
            src_ref=src, dst_ref=dst, send_sem=ssem, recv_sem=rsem, device_id=to, device_id_type=MESH
        )

    first = [share(picked.at[to], got_lon.at[lon], out_sem1.at[to], in_sem1.at[lon], (to, lat)) for to in lons]
    for c in first:
        c.start()
    got_lon[lon] = picked[lon]

    for start in range(0, cells, 256):
        tend = dot(w_last[0], hshift[:, start : start + 256])
        tend += dot(w_last[1], hshift[:, start + 128 : start + 384])
        tend += dot(w_last[2], hshift[:, start + 256 : start + 512])
        for j in range(2):
            r = start // 128 + j
            closing[:, r, :] = wet2s[r] * tend[:, 128 * j : 128 * j + 128]
    closure_out[...] = closing[...].astype(BF16)
    save_closure = pltpu.make_async_copy(closure_out, closure, out_sem.at[0])
    save_closure.start()
    for row in range(count):
        for f in range(3):
            state_out[f, :, row, :] = f_a[row + WIDE, f]
    save_state = pltpu.make_async_copy(state_out, state, out_sem.at[1])
    save_state.start()
    for c, to in zip(first, lons):
        c.wait_send()
        share(picked.at[to], got_lon.at[to], out_sem1.at[to], in_sem1.at[to], (to, lat)).wait_recv()
    got_lat[lat] = jnp.sum(got_lon[...], axis=0)
    second = [share(got_lat.at[lat], got_lat.at[lat], out_sem2.at[to], in_sem2.at[lat], (lon, to)) for to in lats]
    for c in second:
        c.start()
    for c, to in zip(second, lats):
        c.wait_send()
        share(got_lat.at[to], got_lat.at[to], out_sem2.at[to], in_sem2.at[to], (lon, to)).wait_recv()
    chunk[...] = jnp.sum(got_lat[...], axis=0)
    third = [share(chunk, out.at[lon], out_sem3.at[to], in_sem3.at[lon], (to, lat)) for to in lons]
    for c in third:
        c.start()
    save_chunk = pltpu.make_async_copy(chunk, out.at[lon], out_sem.at[2])
    save_chunk.start()
    for c, to in zip(third, lons):
        c.wait_send()
        share(chunk, out.at[to], out_sem3.at[to], in_sem3.at[to], (to, lat)).wait_recv()
    for save in (save_chunk, save_state, save_closure):
        save.wait()


def entry_place(index):
    def parts(value, size):
        whole = jnp.floor((value.astype(F32) + 0.5) * (1.0 / size)).astype(jnp.int32)
        return whole, value - size * whole

    k, rest = parts(index, 1536)
    o, c = parts(rest, 24)
    col = k * 24 + c
    row_f, lane_f = o + 64 * (col >> 7), col & 127
    m = index - 13824
    row_m, lane_m = 128 + (m >> 6), m & 63
    m = index - 17920
    o, col = (m & 1023) >> 6, (m >> 10) * 64 + (m & 63)
    spill = col >= 512
    row_l = jnp.where(spill, 128 + o, 192 + 16 * (col >> 7) + o)
    lane_l = jnp.where(spill, 64 + col - 512, col & 127)
    row = jnp.where(index < 13824, row_f, jnp.where(index < 17920, row_m, row_l))
    lane = jnp.where(index < 13824, lane_f, jnp.where(index < 17920, lane_m, lane_l))
    return row, lane


def on_device(
    n_lon, n_lat, ocean_state, diffusivity, depth_levels, fold_pair, first_weight, mix_weight, last_weight,
    cotangent, active_index,
):
    count = ocean_state.shape[2]
    row_total = count * n_lat
    scale = 1.0 / math.sqrt(row_total * 128 * n_lon)
    sds = jax.ShapeDtypeStruct
    dma = pltpu.SemaphoreType.DMA
    vmem = pltpu.VMEM
    picks = active_index.shape[0] // 128
    depth = picks // n_lon
    total = count + 2 * WIDE
    wide = (count + 4) * 128
    cells = count * 128
    operands = (
        ocean_state, diffusivity, depth_levels, cotangent, fold_pair.reshape(-1, 128),
        jnp.transpose(first_weight, (0, 2, 1)), mix_weight, last_weight, active_index.reshape(picks, 128),
    )
    outs = [
        sds((3, 8, count, 128), F32), sds((16, count, 128), BF16), sds((n_lon, depth, 128), F32),
    ]
    state, closure, reduced = pl.pallas_call(
        functools.partial(kernel, n_lon, n_lat, scale),
        out_shape=outs,
        in_specs=[HBM] * 9,
        out_specs=[ANY] * 3,
        scratch_shapes=[vmem(x.shape, x.dtype) for x in operands] + [
            dma((9,)), vmem((picks, 128), jnp.int32), vmem((picks, 128), jnp.int32), vmem((total, 128), F32),
            vmem((16, 128), BF16), vmem((16, 128), BF16),
            vmem((16, count, 128), F32), vmem((16, count, 128), F32),
            vmem((WIDE, 32, 128), BF16), vmem((WIDE, 32, 128), BF16), vmem((6, 48, 128), BF16),
            vmem((n_lon, 2, 32, 128), BF16), vmem((count, 48, 128), BF16), vmem((48, 128), BF16),
            vmem((n_lon, 128, 256), BF16), vmem((256, picks * 128), BF16),
            vmem((64, 224), BF16), vmem((3, 16, 192), BF16), vmem((64, 144), BF16), vmem((64, 64), BF16),
            vmem((total, 4, 8, 128), F32), vmem((total, 4, 8, 128), F32),
            vmem((total, 3, 8, 128), F32), vmem((total, 3, 8, 128), F32),
            vmem((total, 2, 8, 128), F32), vmem((total, 2, 8, 128), F32),
            vmem((count + 2, 2, 16, 128), F32), vmem((count, 16, 128), F32),
            vmem((224, wide), BF16), vmem((64, wide), F32), vmem((64, wide), F32),
            vmem((64, wide), BF16), vmem((64, wide), F32), vmem((192, (count + 2) * 128), BF16),
            vmem((144, cells), BF16), vmem((64, cells), BF16), vmem((64, cells), BF16),
            vmem((256, 128), F32),
            vmem((n_lon, depth, 128), F32), vmem((n_lon, depth, 128), F32), vmem((n_lat, depth, 128), F32),
            vmem((depth, 128), F32), vmem((3, 8, count, 128), F32), vmem((16, count, 128), BF16), dma((3,)),
            dma((2,)), dma((2,)), dma((2,)), dma((2,)), dma((6,)), dma((6,)), dma((n_lon,)), dma((n_lon,)),
            dma((n_lon,)), dma((n_lon,)), dma((n_lat,)), dma((n_lat,)), dma((n_lon,)), dma((n_lon,)),
        ],
        compiler_params=pltpu.CompilerParams(
            collective_id=0, has_side_effects=True, vmem_limit_bytes=GRANT
        ),
        name="ocean",
    )(*operands)
    return state, closure, reduced.reshape(-1)


def solution(mesh):
    in_specs = (
        P(None, None, "lat", "lon"), P(None, "lat", "lon"), P("lat", "lon"), P(), P(), P(), P(),
        P(None, "lat", "lon"), P(),
    )
    out_specs = (P(None, None, "lat", "lon"), P(None, "lat", "lon"), P())
    return jax.shard_map(
        functools.partial(on_device, mesh.shape["lon"], mesh.shape["lat"]),
        mesh=mesh, in_specs=in_specs, out_specs=out_specs, check_vma=False,
    )
```
